512 devices in a mesh: dp: 32 (over x, z_lo, core), seq: 16 (over y, z_hi).
Axes of the slice: x: 4, y: 8, z: 8 (z_hi: 2, z_lo: 4; z = z_hi * 4 + z_lo), core: 2. Of those that a mesh axis runs over, the one named last changes fastest.
Arguments:
- queries: bfloat16 [32, 2048, 512], P('dp', 'seq'), may hold values from -6 to 6
- keys: bfloat16 [32, 2048, 512], P('dp', 'seq'), may hold values from -6 to 6
- values: bfloat16 [32, 2048, 512], P('dp', 'seq'), may hold values from -30 to 30
- gates: bfloat16 [32, 2048, 512], P('dp', 'seq'), may hold values from -6 to 6
- d_out: bfloat16 [32, 2048, 1024], P('dp', 'seq'), may hold values from -6 to 6
- w_out: bfloat16 [512, 1024], replicated, may hold values from -0.25 to 0.25
- lengths: int32 [32, 4], P('dp'), may hold values from 1 to 1024, 2048 in all within a row
- tile_owner: int32 [32, 16], P('dp'), may hold values from 0 to 15, each once within a row
- pattern: int32 [32, 16, 16], P('dp'), may hold values 0 or 1
Outputs:
- layer_out: bfloat16 [32, 2048, 1024], P('dp', 'seq')
- query_grad: bfloat16 [32, 2048, 512], P('dp', 'seq')
- key_grad: bfloat16 [32, 2048, 512], P('dp', 'seq')
- value_grad: bfloat16 [32, 2048, 512], P('dp', 'seq')
- gate_grad: bfloat16 [32, 2048, 512], P('dp', 'seq')
- weight_grad: float32 [512, 1024], P('dp')
The draws below stay inside these ranges and needn't reach their ends.
Inputs may be any that keep to these rules, and one draw needn't show every extreme that they name: Each group's lengths sum to 2048. `tile_owner`: each group's row is a permutation.
All inputs are finite; a program needn't handle non-finite values. No bound on the sum of `pattern` on one device may be relied on, other than what follows from the above.
Results may differ from the reference program's by a relative error of at most 0.0059.
Values may be sent and summed in bfloat16 or wider, within the bound.
A program may use at most 64 MiB of HBM per device.

```python
import math
import jax
import jax.numpy as jnp
import numpy as np
from jax import lax

D = 1024
H = 4
DH = 128
ATT = 512
ROWS = 128
SEQS = 4
SEQ_ROWS = 2048
N_DP = 32
N_SEQ = 16


def draw_values(key, part):
    key = jax.random.fold_in(key, 11)
    base_key, column_key, row_key = jax.random.split(key, 3)
    draw_shape = (N_DP, SEQ_ROWS, ATT)
    base_draw = jax.random.truncated_normal(base_key, -3.0, 3.0, draw_shape, jnp.float32)
    column_reach = math.log(10.0)
    row_reach = math.log(2.0)
    column_scale = jnp.exp(jax.random.uniform(column_key, (ATT,), jnp.float32, 0.0, column_reach))
    row_scale = jnp.exp(jax.random.uniform(row_key, (N_DP, SEQ_ROWS, 1), jnp.float32, 0.0, row_reach))
    return (base_draw * column_scale * row_scale / 3.0).astype(jnp.bfloat16)


def set_ends(entries, key, smallest, high):
    dims = entries.shape
    index_at = [jax.random.randint(jax.random.fold_in(key, axis), (), 0, dims[axis]) for axis in range(len(dims))]
    entries = entries.at[tuple(index_at)].set(smallest)
    longest = dims.index(max(dims))
    index_at[longest] = (index_at[longest] + 1) % dims[longest]
    return entries.at[tuple(index_at)].set(high)


def level_of(key, shape, shards, least, largest):
    level = 1.0
    for dim, shards_of in shards:
        heights = jax.random.uniform(jax.random.fold_in(jax.random.fold_in(key, 6), dim), (shards_of,), jnp.float32, least / len(shards), largest / len(shards))
        level = level * jnp.repeat(jnp.exp(heights), shape[dim] // shards_of).reshape((-1,) + (1,) * (len(shape) - 1 - dim))
    return level


def split_up(amount, total, most, lean):
    loads = [(1 << 20) // math.isqrt(grade ** lean) + 1 for grade in range(2, amount + 1)]
    rest, given = total - most - (amount - 1), [1] * (amount - 1)
    while rest > 0:
        candidates = [i for i in range(amount - 1) if given[i] < most]
        mass, remaining = sum([loads[i] for i in candidates]), rest
        for i in candidates:
            extra = min(most - given[i], max(1, remaining * loads[i] // mass), rest)
            given[i] = given[i] + extra
            rest = rest - extra
    return np.array([most] + given)


def ragged(rng, amount, total, bound, skew):
    if amount == 2:
        one = jax.random.randint(rng, (), max(1, total - bound), min(bound, total - 1) + 1)
        return jnp.stack([one, total - one])
    sizes = jnp.asarray(split_up(amount, total, bound, skew), jnp.int32)
    twos = (amount - 1) // 2
    donor, receiver = sizes[1:1 + 2 * twos:2], sizes[2:2 + 2 * twos:2]
    room = jnp.minimum(donor - 1, bound - receiver)
    shifted = jax.random.randint(jax.random.fold_in(rng, 1), (twos,), 0, 1 << 20) % (room + 1)
    sizes = sizes.at[1:1 + 2 * twos:2].set(donor - shifted).at[2:2 + 2 * twos:2].set(receiver + shifted)
    return sizes[jax.random.permutation(jax.random.fold_in(rng, 2), amount)]


def scatter_about(own_key, extent, deviation, reach, cuts=(), kind=jnp.bfloat16):
    gain = level_of(own_key, extent, cuts, -0.22, 0.18) if cuts else 1.0
    result = jax.random.normal(own_key, extent, jnp.float32) * deviation * gain
    return jnp.minimum(jnp.maximum(result, -reach), reach).astype(kind)


def setup_inputs(seed: int = 0) -> dict:
    key_of = jax.random.split(jax.random.key(seed), 10)
    queries = scatter_about(key_of[0], (N_DP, SEQ_ROWS, ATT), 1.0, 6.0, ((0, 32), (1, 16)))
    keys = scatter_about(key_of[1], (N_DP, SEQ_ROWS, ATT), 1.0, 6.0, ((0, 32), (1, 16)))
    values = draw_values(jax.random.fold_in(key_of[9], 71), 0)
    gates = scatter_about(key_of[3], (N_DP, SEQ_ROWS, ATT), 1.0, 6.0, ((0, 32), (1, 16)))
    d_out = scatter_about(key_of[4], (N_DP, SEQ_ROWS, D), 1.0, 6.0, ((0, 32), (1, 16)))
    w_out = scatter_about(key_of[5], (ATT, D), ATT ** -0.5, 0.25)
    lengths = jax.vmap(lambda own: ragged(own, SEQS, SEQ_ROWS, SEQ_ROWS // 2, 2))(jax.random.split(key_of[6], N_DP)).reshape((N_DP, SEQS)).astype(jnp.int32)
    tile_owner = jax.vmap(lambda own: jax.random.permutation(own, N_SEQ))(jax.random.split(key_of[7], N_DP)).reshape((N_DP, N_SEQ)).astype(jnp.int32)
    pattern = set_ends((jax.random.randint(key_of[8], (N_DP, N_SEQ, N_SEQ), 0, 2) < 1).astype(jnp.int32), jax.random.fold_in(key_of[8], 1), 0, 1)
    return dict(queries=queries, keys=keys, values=values, gates=gates, d_out=d_out, w_out=w_out, lengths=lengths, tile_owner=tile_owner, pattern=pattern)


eps = 1e-06

def positions(row_index, owner_row, tile_rows):
    slot_ids = jnp.arange(owner_row.shape[0], dtype=jnp.int32)
    inverse = lax.optimization_barrier(jnp.sum(jnp.where(owner_row[:, None] == slot_ids[None, :], slot_ids[:, None], 0), axis=0, dtype=jnp.int32))
    device_of = row_index // tile_rows
    tile_of = lax.optimization_barrier(jnp.sum(jnp.where(device_of[:, None] == slot_ids[None, :], inverse[None, :], 0), axis=1, dtype=jnp.int32))
    return (tile_of, tile_of * tile_rows + row_index % tile_rows)

def users_of(position, user_lengths):
    user_ends = jnp.cumsum(user_lengths, dtype=jnp.int32)
    return lax.optimization_barrier(jnp.sum((position[:, None] >= user_ends[None, :]).astype(jnp.int32), axis=1, dtype=jnp.int32))

def describe(row_index, owner_row, user_lengths, tile_rows):
    tile_of, position = positions(row_index, owner_row, tile_rows)
    return (tile_of, position, users_of(position, user_lengths))

def block_mask(query_side, key_side, link_table):
    query_tiles, query_pos, query_users = query_side
    key_tiles, key_pos, key_users = key_side
    slot_ids = jnp.arange(link_table.shape[0], dtype=jnp.int32)
    query_hot = (query_tiles[:, None] == slot_ids[None, :]).astype(link_table.dtype)
    key_hot = (key_tiles[:, None] == slot_ids[None, :]).astype(link_table.dtype)
    linked = jnp.dot(jnp.dot(query_hot, link_table), key_hot.T)
    keep = (query_users[:, None] == key_users[None, :]) & (key_pos[None, :] <= query_pos[:, None])
    keep = keep & ((query_tiles[:, None] == key_tiles[None, :]) | (linked > 0.5))
    return keep.astype(jnp.float32)

def silu_slope(scores):
    sig_scores = jax.nn.sigmoid(scores)
    return sig_scores * (1.0 + scores * (1.0 - sig_scores))

def one_column(operands, w_out):
    query_rows, key_rows, value_rows, gate_rows, out_grad, user_lengths, owner_row, link_raw = operands
    row_total = query_rows.shape[0]
    row_index = jnp.arange(row_total, dtype=jnp.int32)
    side = describe(row_index, owner_row, user_lengths, ROWS)
    keep_mask = block_mask(side, side, link_raw.astype(jnp.float32))
    score_scale = DH ** (-0.5)
    query_f = query_rows.astype(jnp.float32).reshape(row_total, H, DH)
    key_f = key_rows.astype(jnp.float32).reshape(row_total, H, DH)
    value_f = value_rows.astype(jnp.float32).reshape(row_total, H, DH)
    scores = jnp.einsum('qhd,khd->hqk', query_f, key_f) * score_scale
    weights = (jax.nn.silu(scores) * keep_mask).astype(jnp.bfloat16)
    attended = jnp.einsum('hqk,khd->qhd', weights.astype(jnp.float32), value_f).reshape(row_total, ATT)
    row_mean = lax.optimization_barrier(jnp.mean(attended, axis=1, keepdims=True))
    centred = attended - row_mean
    inv_std = lax.rsqrt(lax.optimization_barrier(jnp.mean(centred * centred, axis=1, keepdims=True)) + eps)
    normed = centred * inv_std
    gates_f = gate_rows.astype(jnp.float32)
    gated = (normed * gates_f).astype(jnp.bfloat16)
    layer_out = jnp.dot(gated, w_out, preferred_element_type=jnp.float32).astype(jnp.bfloat16)
    d_gated = lax.dot_general(out_grad, w_out, (((1,), (1,)), ((), ())), preferred_element_type=jnp.float32)
    weight_part = lax.dot_general(gated, out_grad, (((0,), (0,)), ((), ())), preferred_element_type=jnp.float32)
    gate_grad = (d_gated * normed).astype(jnp.bfloat16)
    d_normed = d_gated * gates_f
    d_center = d_normed - lax.optimization_barrier(jnp.mean(d_normed, axis=1, keepdims=True))
    d_attended = ((d_center - normed * lax.optimization_barrier(jnp.mean(d_normed * normed, axis=1, keepdims=True))) * inv_std).astype(jnp.bfloat16)
    d_att_f = d_attended.astype(jnp.float32).reshape(row_total, H, DH)
    d_weights = jnp.einsum('qhd,khd->hqk', d_att_f, value_f)
    d_scores = (d_weights * silu_slope(scores) * keep_mask * score_scale).astype(jnp.bfloat16)
    d_scores_f = d_scores.astype(jnp.float32)
    query_grad = jnp.einsum('hqk,khd->qhd', d_scores_f, key_f).reshape(row_total, ATT).astype(jnp.bfloat16)
    key_grad = jnp.einsum('hqk,qhd->khd', d_scores_f, query_f).reshape(row_total, ATT).astype(jnp.bfloat16)
    value_grad = jnp.einsum('hqk,qhd->khd', weights.astype(jnp.float32), d_att_f).reshape(row_total, ATT).astype(jnp.bfloat16)
    return (layer_out, query_grad, key_grad, value_grad, gate_grad, weight_part)

def reference(queries, keys, values, gates, d_out, w_out, lengths, tile_owner, pattern):

    def step_column(weight_sum, operands):
        layer_out, query_grad, key_grad, value_grad, gate_grad, weight_part = one_column(operands, w_out)
        return (weight_sum + weight_part, (layer_out, query_grad, key_grad, value_grad, gate_grad))
    start_sum = jnp.zeros((ATT, D), jnp.float32)
    weight_grad, stacked = lax.scan(step_column, start_sum, (queries, keys, values, gates, d_out, lengths, tile_owner, pattern))
    layer_out, query_grad, key_grad, value_grad, gate_grad = stacked
    return (layer_out, query_grad, key_grad, value_grad, gate_grad, weight_grad)
```

```python
import functools

import jax
import jax.numpy as jnp
from jax import lax
from jax.experimental import pallas as pl
from jax.experimental.pallas import tpu as pltpu
from jax.sharding import PartitionSpec as P

H = 4
DH = 128
T = 128
F32 = jnp.float32
BF16 = jnp.bfloat16
MESH = pl.DeviceIdType.MESH
EPS = 1e-06
NT = (((1,), (1,)), ((), ()))
TN = (((0,), (0,)), ((), ()))
HALF_SCALE = 0.5 * DH ** (-0.5)


def dot(a, b, dims=(((1,), (0,)), ((), ()))):
    return lax.dot_general(a, b, dims, preferred_element_type=F32)


def kernel(
    q_ref, k_ref, v_ref, g_ref, do_ref, w_ref, len_ref, own_ref, pat_ref,
    lo_ref, dq_ref, dk_ref, dv_ref, gg_ref, wg_ref,
    kv_s, q_s, meta_s, meta_r, kv, rq, kt, wt, sl, low, high, att_t, att_s, ratt,
    dgat, gated, da_s, rda, sib_s, sib_r, dkv_s, rdkv, dq_t, dq_s, rdq,
    do_sib, g_t, g_sib, wx_own, wx_s, wx_r, wl_s, wl_r, ws, ws_r, wa_s, wa,
    kv_send, kv_recv, fwd_send, q_send, q_recv, one_send, one_recv, att_send, att_recv,
    da_send, da_recv, sib_send, sib_recv, dkv_send, dkv_recv, dq_send, dq_recv,
    x_send, x_recv, l_send, l_recv, s_send, s_recv, a_send, a_recv,
):
    dp = lax.axis_index("dp")
    sq = lax.axis_index("seq")
    x = lax.div(dp, 8)
    l = lax.rem(lax.div(dp, 2), 4)
    c = lax.rem(dp, 2)
    y = lax.div(sq, 2)
    z = lax.rem(sq, 2)
    par = lax.rem(y, 2)
    hh = lax.div(y, 2)
    sib = (dp + 1 - 2 * c, sq)
    own_par = par == c

    def partner(k, zz):
        return (dp - c + par, (2 * k + c) * 2 + zz)

    def is_self(k, zz):
        return own_par & (k == hh) & (zz == z)

    def remote(src, dst, send, recv, to):
        return pltpu.make_async_remote_copy(
            src_ref=src, dst_ref=dst, send_sem=send, recv_sem=recv, device_id=to,
            device_id_type=MESH,
        )

    def arrived(dst, sem):
        pltpu.make_async_copy(dst, dst, sem).wait()

    def push(src, dst, send, recv, k, zz):
        me = is_self(k, zz)

        @pl.when(jnp.logical_not(me))
        def _():
            remote(src, dst, send, recv, partner(k, zz)).start()

        @pl.when(me)
        def _():
            pltpu.make_async_copy(src, dst, recv).start()

    def pushed(src, dst, send, recv, k, zz):
        @pl.when(jnp.logical_not(is_self(k, zz)))
        def _():
            remote(src, dst, send, recv, partner(k, zz)).wait_send()

    def x_dev(i):
        return (lax.rem(x + i, 4) * 8 + l * 2 + c, sq)

    def l_dev(i):
        return (x * 8 + lax.rem(l + i, 4) * 2 + c, sq)

    def s_dev(i):
        return (dp, lax.rem(sq + i, 16))

    barrier = pltpu.get_barrier_semaphore()

    def tell(to):
        pl.semaphore_signal(barrier, inc=1, device_id=to, device_id_type=MESH)

    for k in range(4):
        for zz in range(2):
            @pl.when(jnp.logical_not(is_self(k, zz)))
            def _():
                tell(partner(k, zz))
    tell(sib)
    for i in range(1, 4):
        tell(x_dev(i))
        tell(l_dev(i))
    for i in range(1, 16):
        tell(s_dev(i))

    for h in range(H):
        cols = slice(h * DH, (h + 1) * DH)
        kv_s[h, 0] = k_ref[0, :, cols]
        kv_s[h, 1] = v_ref[0, :, cols]
        q_s[h] = q_ref[0, :, cols]
    meta_s[...] = jnp.zeros_like(meta_s)
    meta_s[0:1, 0:4] = len_ref[...].astype(F32)
    meta_s[1:2, 0:16] = own_ref[...].astype(F32)
    meta_s[8:24, 0:16] = pat_ref[0].astype(F32)

    pl.semaphore_wait(barrier, 30 - jnp.where(own_par, 1, 0))

    meta_copy = remote(meta_s, meta_r, one_send.at[0], one_recv.at[0], sib)
    meta_copy.start()

    def place(i):
        step = lax.rem(i, 4)
        turn = jnp.where(step == 2, 3, jnp.where(step == 3, 2, step))
        return lax.rem(hh + turn, 4), jnp.where(i < 4, z, 1 - z)

    for k in range(4):
        push(q_s.at[k], rq.at[hh], q_send.at[k], q_recv.at[hh], k, z)
    for zz in (1 - z, z):
        for k in range(4):
            push(kv_s.at[k], kv.at[sq], kv_send.at[2 * k + zz], kv_recv.at[sq], k, zz)
    do_copy = remote(do_ref.at[0], do_sib, one_send.at[1], one_recv.at[1], sib)
    do_copy.start()

    dgat[...] = dot(do_ref[0], w_ref[...], NT)

    meta_copy.wait()
    meta = jnp.where(own_par, meta_s[...], meta_r[...])
    lane = lax.broadcasted_iota(jnp.int32, (16, 128), 1).astype(F32)
    seat = lax.broadcasted_iota(jnp.int32, (16, 128), 0).astype(F32)
    hot = jnp.where((meta[1:2] == seat) & (lane < 16), 1.0, 0.0)
    tile = jnp.sum(hot * lane, axis=1, keepdims=True)
    col = lax.broadcasted_iota(jnp.int32, (16, 512), 1)
    row = lax.broadcasted_iota(jnp.int32, (16, 512), 0)
    query_hot = jnp.where(row == 4 * lax.div(col, 128) + 2 * c + z, 1.0, 0.0)
    query_tile = jnp.sum(tile * query_hot, axis=0, keepdims=True)
    pos = query_tile * T + lax.rem(col, 128)[0:1].astype(F32)
    lengths = jnp.where((lane[0:8] <= seat[0:8]) & (lane[0:8] < 4), meta[0:1], 0.0)
    ends = jnp.sum(lengths, axis=1, keepdims=True)
    first = jnp.max(jnp.where(ends <= pos, ends, 0.0), axis=0, keepdims=True)
    tile_hot = jnp.where(row.astype(F32) == query_tile, 1.0, 0.0)
    seen = dot(meta[8:24], tile_hot, TN)
    allow = (dot(hot, seen) > 0.5) | (tile == query_tile)
    low[...] = jnp.where(allow, first - tile * T, 1e6)
    high[...] = pos - tile * T

    for k in range(4):
        arrived(rq.at[k], q_recv.at[k])

    att_t[...] = jnp.zeros_like(att_t)

    def attend(s):
        keys = kv[s, 0]
        values_t = kv[s, 1].T
        kt[s] = keys.T
        key_at = lax.broadcasted_iota(jnp.int32, (T, 256), 0).astype(F32)
        for j in range(2):
            cols = slice(j * 256, (j + 1) * 256)
            part = dot(keys, rq[2 * j : 2 * j + 2].reshape(256, DH), NT) * HALF_SCALE
            keep = (key_at >= low[pl.ds(s, 1), cols]) & (key_at <= high[pl.ds(s, 1), cols])
            tan = jnp.tanh(part)
            up = 1.0 + tan
            weights = jnp.where(keep, part * up, 0.0).astype(BF16)
            slope = up * (1.0 + part * (1.0 - tan)) * HALF_SCALE
            wt[s, :, cols] = weights
            sl[s, :, cols] = jnp.where(keep, slope, 0.0)
            att_t[:, cols] += dot(values_t, weights)

    def forward_step(i, _):
        k, zz = place(i)
        mine = (2 * k + c) * 2 + zz
        arrived(kv.at[mine], kv_recv.at[mine])
        remote(kv.at[mine], kv.at[mine], fwd_send.at[i], kv_recv.at[mine], sib).start()
        attend(mine)
        other = (2 * k + 1 - c) * 2 + zz
        arrived(kv.at[other], kv_recv.at[other])
        attend(other)
        return 0

    lax.fori_loop(0, 8, forward_step, 0)

    for k in range(4):
        att_s[k] = att_t[:, k * T : (k + 1) * T].T
        push(att_s.at[k], ratt.at[hh], att_send.at[k], att_recv.at[hh], k, z)

    for h in range(H):
        arrived(ratt.at[h], att_recv.at[h])
    rows = [ratt[h] for h in range(H)]
    mean = sum(jnp.sum(r, axis=1, keepdims=True) for r in rows) * (1.0 / 512)
    rows = [r - mean for r in rows]
    var = sum(jnp.sum(r * r, axis=1, keepdims=True) for r in rows) * (1.0 / 512)
    inv = lax.rsqrt(var + EPS)
    normed = [r * inv for r in rows]
    d_normed = []
    for h in range(H):
        cols = slice(h * DH, (h + 1) * DH)
        gates = g_ref[0, :, cols].astype(F32)
        d_gated = dgat[:, cols]
        gated[:, cols] = (normed[h] * gates).astype(BF16)
        gg_ref[0, :, cols] = (d_gated * normed[h]).astype(BF16)
        d_normed.append(d_gated * gates)
    mean_d = sum(jnp.sum(d, axis=1, keepdims=True) for d in d_normed) * (1.0 / 512)
    mean_dn = sum(
        jnp.sum(d * n, axis=1, keepdims=True) for d, n in zip(d_normed, normed)
    ) * (1.0 / 512)
    for h in range(H):
        da_s[h] = ((d_normed[h] - mean_d - normed[h] * mean_dn) * inv).astype(BF16)
        push(da_s.at[h], rda.at[hh], da_send.at[h], da_recv.at[hh], h, z)

    for h in range(H):
        g_t[4 * h : 4 * h + 4] = gated[:, h * DH : (h + 1) * DH].T.reshape(4, 2, 16, T)
    g_copy = remote(g_t.at[:, 1 - c], g_sib, one_send.at[2], one_recv.at[2], sib)
    g_copy.start()
    lo_ref[0] = dot(gated[...], w_ref[...]).astype(BF16)
    do_copy.wait()
    g_copy.wait()
    mine_t = g_t[:, pl.ds(c, 1)].reshape(256, T)
    theirs_t = g_sib[...].reshape(256, T)
    part = dot(mine_t, do_ref[0]) + dot(theirs_t, do_sib[...])
    wx_own[...] = part.reshape(4, 64, 1024)
    wx_s[...] = part.astype(BF16).reshape(4, 64, 1024)
    for i in range(1, 4):
        there = lax.rem(x + i, 4)
        remote(wx_s.at[there], wx_r.at[i - 1], x_send.at[i - 1], x_recv.at[i - 1], x_dev(i)).start()

    for k in range(4):
        arrived(rda.at[k], da_recv.at[k])
    dq_t[...] = jnp.zeros_like(dq_t)

    def back(s):
        values = kv[s, 1]
        d_keys = jnp.zeros((T, DH), F32)
        d_values = jnp.zeros((T, DH), F32)
        for j in range(2):
            cols = slice(j * 256, (j + 1) * 256)
            grads = rda[2 * j : 2 * j + 2].reshape(256, DH)
            d_scores = (dot(values, grads, NT) * sl[s, :, cols]).astype(BF16)
            d_keys += dot(d_scores, rq[2 * j : 2 * j + 2].reshape(256, DH))
            d_values += dot(wt[s, :, cols], grads)
            dq_t[:, cols] += dot(kt[s], d_scores)
        return d_keys, d_values

    def back_other(i, _):
        k, zz = place(7 - i)
        d_keys, d_values = back((2 * k + 1 - c) * 2 + zz)
        sib_s[i, 0] = d_keys.astype(BF16)
        sib_s[i, 1] = d_values.astype(BF16)
        remote(sib_s.at[i], sib_r.at[i], sib_send.at[i], sib_recv.at[i], sib).start()
        return 0

    def back_mine(i, _):
        k, zz = place(7 - i)
        d_keys, d_values = back((2 * k + c) * 2 + zz)
        arrived(sib_r.at[i], sib_recv.at[i])
        dkv_s[i, 0] = (d_keys + sib_r[i, 0].astype(F32)).astype(BF16)
        dkv_s[i, 1] = (d_values + sib_r[i, 1].astype(F32)).astype(BF16)
        push(dkv_s.at[i], rdkv.at[z, hh], dkv_send.at[i], dkv_recv.at[4 * z + hh], k, zz)
        return 0

    lax.fori_loop(0, 8, back_other, 0)
    lax.fori_loop(0, 8, back_mine, 0)
    for k in range(4):
        dq_s[k] = dq_t[:, k * T : (k + 1) * T].T.astype(BF16)
        push(dq_s.at[k], rdq.at[hh], dq_send.at[k], dq_recv.at[hh], k, z)

    for i in range(3):
        arrived(wx_r.at[i], x_recv.at[i])
    total = wx_own[x]
    for i in range(3):
        total += wx_r[i].astype(F32)
    wl_s[...] = total.reshape(4, 16, 1024)
    for i in range(1, 4):
        there = lax.rem(l + i, 4)
        remote(wl_s.at[there], wl_r.at[i - 1], l_send.at[i - 1], l_recv.at[i - 1], l_dev(i)).start()
    for i in range(3):
        arrived(wl_r.at[i], l_recv.at[i])
    ws[...] = wl_s[l] + wl_r[0] + wl_r[1] + wl_r[2]

    def piece(ref, s):
        down = pl.multiple_of(lax.div(s, 8) * 8, 8)
        across = pl.multiple_of(lax.rem(s, 8) * 128, 128)
        return ref.at[pl.ds(down, 8), pl.ds(across, 128)]

    def spread(i, _):
        there = lax.rem(sq + i, 16)
        remote(piece(ws, there), ws_r.at[i], s_send.at[i], s_recv.at[i], s_dev(i)).start()
        return 0

    lax.fori_loop(1, 16, spread, 0)
    pltpu.make_async_copy(piece(ws, sq), ws_r.at[0], s_recv.at[0]).start()

    def fold(i, acc):
        arrived(ws_r.at[i], s_recv.at[i])
        return acc + ws_r[i]

    wa_s[...] = lax.fori_loop(0, 16, fold, jnp.zeros((8, 128), F32))

    def share(i, _):
        remote(wa_s, piece(wa, sq), a_send.at[i], a_recv.at[sq], s_dev(i)).start()
        return 0

    lax.fori_loop(1, 16, share, 0)
    pltpu.make_async_copy(wa_s, piece(wa, sq), a_recv.at[sq]).start()

    for h in range(H):
        cols = slice(h * DH, (h + 1) * DH)
        arrived(rdq.at[h], dq_recv.at[h])
        dq_ref[0, :, cols] = rdq[h]
    for h in range(H):
        cols = slice(h * DH, (h + 1) * DH)
        arrived(rdkv.at[0, h], dkv_recv.at[h])
        arrived(rdkv.at[1, h], dkv_recv.at[4 + h])
        dk_ref[0, :, cols] = (rdkv[0, h, 0].astype(F32) + rdkv[1, h, 0].astype(F32)).astype(BF16)
        dv_ref[0, :, cols] = (rdkv[0, h, 1].astype(F32) + rdkv[1, h, 1].astype(F32)).astype(BF16)

    def gathered(i, _):
        arrived(piece(wa, i), a_recv.at[i])
        return 0

    lax.fori_loop(0, 16, gathered, 0)
    wg_ref[...] = wa[...]

    for k in range(4):
        pushed(q_s.at[k], rq.at[hh], q_send.at[k], q_recv.at[hh], k, z)
        pushed(att_s.at[k], ratt.at[hh], att_send.at[k], att_recv.at[hh], k, z)
        pushed(da_s.at[k], rda.at[hh], da_send.at[k], da_recv.at[hh], k, z)
        pushed(dq_s.at[k], rdq.at[hh], dq_send.at[k], dq_recv.at[hh], k, z)
        for zz in range(2):
            pushed(kv_s.at[k], kv.at[sq], kv_send.at[2 * k + zz], kv_recv.at[sq], k, zz)

    def left(i, _):
        k, zz = place(i)
        mine = (2 * k + c) * 2 + zz
        remote(kv.at[mine], kv.at[mine], fwd_send.at[i], kv_recv.at[mine], sib).wait_send()
        remote(sib_s.at[i], sib_r.at[i], sib_send.at[i], sib_recv.at[i], sib).wait_send()
        k, zz = place(7 - i)
        pushed(dkv_s.at[i], rdkv.at[z, hh], dkv_send.at[i], dkv_recv.at[4 * z + hh], k, zz)
        return 0

    lax.fori_loop(0, 8, left, 0)
    for i in range(1, 4):
        remote(wx_s.at[i], wx_r.at[i - 1], x_send.at[i - 1], x_recv.at[i - 1], x_dev(i)).wait_send()
        remote(wl_s.at[i], wl_r.at[i - 1], l_send.at[i - 1], l_recv.at[i - 1], l_dev(i)).wait_send()

    def left_seq(i, _):
        remote(wa_s, ws_r.at[i], s_send.at[i], s_recv.at[i], s_dev(i)).wait_send()
        remote(wa_s, ws_r.at[i], a_send.at[i], a_recv.at[i], s_dev(i)).wait_send()
        return 0

    lax.fori_loop(1, 16, left_seq, 0)


def body(queries, keys, values, gates, d_out, w_out, lengths, tile_owner, pattern):
    vmem = pl.BlockSpec(memory_space=pltpu.VMEM)
    rows = jax.ShapeDtypeStruct((1, T, 512), BF16)
    dma = pltpu.SemaphoreType.DMA
    buf = pltpu.VMEM
    scratch = dict(
        kv_s=buf((4, 2, T, DH), BF16), q_s=buf((4, T, DH), BF16),
        meta_s=buf((24, 128), F32), meta_r=buf((24, 128), F32),
        kv=buf((16, 2, T, DH), BF16), rq=buf((4, T, DH), BF16), kt=buf((16, DH, T), BF16),
        wt=buf((16, T, 512), BF16), sl=buf((16, T, 512), F32),
        low=buf((16, 512), F32), high=buf((16, 512), F32),
        att_t=buf((DH, 512), F32), att_s=buf((4, T, DH), F32), ratt=buf((4, T, DH), F32),
        dgat=buf((T, 512), F32), gated=buf((T, 512), BF16),
        da_s=buf((4, T, DH), BF16), rda=buf((4, T, DH), BF16),
        sib_s=buf((8, 2, T, DH), BF16), sib_r=buf((8, 2, T, DH), BF16),
        dkv_s=buf((8, 2, T, DH), BF16), rdkv=buf((2, 4, 2, T, DH), BF16),
        dq_t=buf((DH, 512), F32), dq_s=buf((4, T, DH), BF16), rdq=buf((4, T, DH), BF16),
        do_sib=buf((T, 1024), BF16), g_t=buf((16, 2, 16, T), BF16), g_sib=buf((16, 16, T), BF16),
        wx_own=buf((4, 64, 1024), F32), wx_s=buf((4, 64, 1024), BF16), wx_r=buf((3, 64, 1024), BF16),
        wl_s=buf((4, 16, 1024), F32), wl_r=buf((3, 16, 1024), F32),
        ws=buf((16, 1024), F32), ws_r=buf((16, 8, 128), F32),
        wa_s=buf((8, 128), F32), wa=buf((16, 1024), F32),
        kv_send=dma((8,)), kv_recv=dma((16,)), fwd_send=dma((8,)), q_send=dma((4,)), q_recv=dma((4,)),
        one_send=dma((3,)), one_recv=dma((3,)), att_send=dma((4,)), att_recv=dma((4,)),
        da_send=dma((4,)), da_recv=dma((4,)), sib_send=dma((8,)), sib_recv=dma((8,)),
        dkv_send=dma((8,)), dkv_recv=dma((8,)), dq_send=dma((4,)), dq_recv=dma((4,)),
        x_send=dma((3,)), x_recv=dma((3,)), l_send=dma((3,)), l_recv=dma((3,)),
        s_send=dma((16,)), s_recv=dma((16,)), a_send=dma((16,)), a_recv=dma((16,)),
    )
    return pl.pallas_call(
        kernel,
        out_shape=(
            jax.ShapeDtypeStruct((1, T, 1024), BF16), rows, rows, rows, rows,
            jax.ShapeDtypeStruct((16, 1024), F32),
        ),
        in_specs=[vmem] * 9,
        out_specs=(vmem,) * 6,
        scratch_shapes=list(scratch.values()),
        name="hstu",
        compiler_params=pltpu.CompilerParams(
            collective_id=0, has_side_effects=True, vmem_limit_bytes=48 << 20
        ),
    )(queries, keys, values, gates, d_out, w_out, lengths, tile_owner, pattern)


def solution(mesh):
    rows = P("dp", "seq", None)
    in_specs = (rows, rows, rows, rows, rows, P(), P("dp", None), P("dp", None), P("dp", None, None))
    out_specs = (rows, rows, rows, rows, rows, P("dp", None))
    return jax.shard_map(body, mesh=mesh, in_specs=in_specs, out_specs=out_specs, check_vma=False)
```

```python
import jax
import jax.numpy as jnp
from jax import lax
from jax.experimental import pallas as pl
from jax.experimental.pallas import tpu as pltpu
from jax.sharding import PartitionSpec as P

H = 4
DH = 128
T = 128
F32 = jnp.float32
BF16 = jnp.bfloat16
MESH = pl.DeviceIdType.MESH
EPS = 1e-06
NT = (((1,), (1,)), ((), ()))
TN = (((0,), (0,)), ((), ()))
VMEM = 60 << 20
HALF_SCALE = 0.5 * DH ** (-0.5)


def dot(a, b, dims=(((1,), (0,)), ((), ()))):
    return lax.dot_general(a, b, dims, preferred_element_type=F32)


def kernel(
    q_ref, k_ref, v_ref, g_ref, do_ref, w_ref, len_ref, own_ref, pat_ref,
    lo_out, dq_out, dk_out, dv_out, gg_out, wg_out,
    lo_v, dq_v, dk_v, dv_v, gg_v, kv_s, q_s, g_v, w_v, len_v, own_v, pat_v,
    meta_s, meta_r, kv, rq, kt, wt, sl, low, high, att_t, att_s, ratt,
    dgat, gate_t, gated_t, gg_t, da_s, rda, dkv_f, sib_s, sib_r, dkv_s, rdkv, dq_t, dq_s, rdq,
    dox, g_t, gx, wl_f, wl_s, wl_r, ws, ws_r, wa_s, wa,
    in_sem, out_sem, kv_send, kv_recv, fwd_send, q_send, q_recv, meta_sem, att_send, att_recv,
    da_send, da_recv, sib_send, sib_recv, dkv_send, dkv_recv, dq_send, dq_recv,
    do_send, do_recv, g_send, g_recv, l_send, l_recv, s_send, s_recv, a_send, a_recv,
):
    dp = lax.axis_index("dp")
    sq = lax.axis_index("seq")
    x = lax.div(dp, 8)
    l = lax.rem(lax.div(dp, 2), 4)
    c = lax.rem(dp, 2)
    y = lax.div(sq, 2)
    z = lax.rem(sq, 2)
    par = lax.rem(y, 2)
    hh = lax.div(y, 2)
    xc = x * 2 + c
    sib = (dp + 1 - 2 * c, sq)
    own_par = par == c
    own_rows = pl.ds(pl.multiple_of(c * T, T), T)
    sib_rows = pl.ds(pl.multiple_of((1 - c) * T, T), T)
    my_rows = pl.ds(pl.multiple_of(par * T, T), T)

    def partner(k, far):
        return (dp - c + par, (2 * k + c) * 2 + jnp.where(far, 1 - z, z))

    def is_self(k, far):
        return own_par & (k == hh) & jnp.logical_not(far)

    def remote(src, dst, send, recv, to):
        return pltpu.make_async_remote_copy(
            src_ref=src, dst_ref=dst, send_sem=send, recv_sem=recv, device_id=to,
            device_id_type=MESH,
        )

    def arrived(dst, sem):
        pltpu.make_async_copy(dst, dst, sem).wait()

    def push(src, dst, send, recv, k, far=False):
        if far is True:
            remote(src, dst, send, recv, partner(k, far)).start()
            return
        me = is_self(k, far)

        @pl.when(jnp.logical_not(me))
        def _():
            remote(src, dst, send, recv, partner(k, far)).start()

        @pl.when(me)
        def _():
            pltpu.make_async_copy(src, dst, recv).start()

    def pushed(src, dst, send, recv, k, far=False):
        @pl.when(jnp.logical_not(is_self(k, far)))
        def _():
            remote(src, dst, send, recv, partner(k, far)).wait_send()

    def x_dev(i, cc):
        return (lax.rem(x + i, 4) * 8 + l * 2 + cc, sq)

    def l_dev(i):
        return (x * 8 + lax.rem(l + i, 4) * 2 + c, sq)

    def s_dev(i):
        return (dp, lax.rem(sq + i, 16))

    loads = []

    def load(src, dst):
        copy = pltpu.make_async_copy(src, dst, in_sem.at[len(loads)])
        copy.start()
        loads.append(copy)

    load(len_ref, len_v)
    load(own_ref, own_v)
    load(pat_ref, pat_v)
    for h in range(H):
        cols = pl.ds(h * DH, DH)
        load(q_ref.at[0, :, cols], q_s.at[h])
        load(k_ref.at[0, :, cols], kv_s.at[h, 0])
        load(v_ref.at[0, :, cols], kv_s.at[h, 1])
    load(do_ref.at[0], dox.at[xc])
    load(w_ref, w_v)
    load(g_ref.at[0], g_v)

    barrier = pltpu.get_barrier_semaphore()

    def tell(to):
        pl.semaphore_signal(barrier, inc=1, device_id=to, device_id_type=MESH)

    for k in range(4):
        tell(partner(k, True))
        @pl.when(jnp.logical_not(is_self(k, False)))
        def _():
            tell(partner(k, False))
    tell(sib)
    for i in range(1, 4):
        tell(x_dev(i, c))
        tell(x_dev(i, 1 - c))
        tell(l_dev(i))
    for i in range(1, 16):
        tell(s_dev(i))

    for copy in loads[:3]:
        copy.wait()
    meta_s[...] = jnp.zeros_like(meta_s)
    meta_s[0:1, 0:4] = len_v[...].astype(F32)
    meta_s[1:2, 0:16] = own_v[...].astype(F32)
    meta_s[8:24, 0:16] = pat_v[0].astype(F32)
    for copy in loads[3:15]:
        copy.wait()

    pl.semaphore_wait(barrier, 33 - jnp.where(own_par, 1, 0))

    meta_copy = remote(meta_s, meta_r, meta_sem.at[0], meta_sem.at[1], sib)
    meta_copy.start()
    for k in range(4):
        push(q_s.at[k], rq.at[hh], q_send.at[k], q_recv.at[hh], k)
    for k in range(4):
        push(kv_s.at[k], kv.at[4 + hh, :, my_rows], kv_send.at[4 + k], kv_recv.at[8 + y], k, True)
        push(kv_s.at[k], kv.at[hh, :, my_rows], kv_send.at[k], kv_recv.at[y], k)
    for copy in loads[15:]:
        copy.wait()
    remote(dox.at[xc], dox.at[xc], do_send.at[0], do_recv.at[xc], sib).start()
    for i in range(1, 4):
        remote(dox.at[xc], dox.at[xc], do_send.at[i], do_recv.at[xc], x_dev(i, c)).start()

    def place(i):
        step = lax.rem(i, 4)
        turn = jnp.where(step == 2, 3, jnp.where(step == 3, 2, step))
        return lax.rem(hh + turn, 4), lax.div(i, 4)

    dgat[...] = dot(w_v[...], dox[xc], NT)
    for h in range(H):
        gate_t[h * DH : (h + 1) * DH] = g_v[:, h * DH : (h + 1) * DH].T

    meta_copy.wait()
    meta = jnp.where(own_par, meta_s[...], meta_r[...])
    lane = lax.broadcasted_iota(jnp.int32, (16, 128), 1).astype(F32)
    slot = lax.broadcasted_iota(jnp.int32, (16, 128), 0)
    seat = (2 * lax.rem(slot, 8) + jnp.where(slot < 8, z, 1 - z)).astype(F32)
    hot = jnp.where((meta[1:2] == seat) & (lane < 16), 1.0, 0.0)
    tile = jnp.sum(hot * lane, axis=1, keepdims=True)
    col = lax.broadcasted_iota(jnp.int32, (16, 512), 1)
    row = lax.broadcasted_iota(jnp.int32, (16, 512), 0)
    query_hot = jnp.where(row == 2 * lax.div(col, 128) + c, 1.0, 0.0)
    query_tile = jnp.sum(tile * query_hot, axis=0, keepdims=True)
    pos = query_tile * T + lax.rem(col, 128)[0:1].astype(F32)
    upto = slot[0:8].astype(F32)
    lengths = jnp.where((lane[0:8] <= upto) & (lane[0:8] < 4), meta[0:1], 0.0)
    ends = jnp.sum(lengths, axis=1, keepdims=True)
    first = jnp.max(jnp.where(ends <= pos, ends, 0.0), axis=0, keepdims=True)
    tile_hot = jnp.where(row.astype(F32) == query_tile, 1.0, 0.0)
    seen = dot(meta[8:24], tile_hot, TN)
    allow = (dot(hot, seen) > 0.5) | (tile == query_tile)
    low[...] = jnp.where(allow, first - tile * T, 1e6)
    high[...] = pos - tile * T

    for k in range(4):
        arrived(rq.at[k], q_recv.at[k])

    att_t[...] = jnp.zeros_like(att_t)

    def hand_on(i):
        k, far = place(i)
        here = kv.at[4 * far + k, :, own_rows]
        u = 8 * far + 2 * k + c
        arrived(here, kv_recv.at[u])
        remote(here, here, fwd_send.at[i], kv_recv.at[u], sib).start()

    def attend(i):
        k, far = place(i)
        p = 4 * far + k
        u = 8 * far + 2 * k
        arrived(kv.at[p, :, sib_rows], kv_recv.at[u + 1 - c])
        keys = kv[p, 0]
        values_t = kv[p, 1].T
        kt[p] = keys.T
        key_at = lax.broadcasted_iota(jnp.int32, (T, 256), 0).astype(F32)
        for j in range(2):
            cols = slice(j * 256, (j + 1) * 256)
            part = dot(keys, rq[2 * j : 2 * j + 2].reshape(256, DH), NT) * HALF_SCALE
            tan = jnp.tanh(part)
            up = 1.0 + tan
            weights = part * up
            slope = up * (HALF_SCALE + (part * HALF_SCALE) * (1.0 - tan))
            for m in range(2):
                half = slice(m * T, (m + 1) * T)
                keep = (key_at >= low[pl.ds(u + m, 1), cols]) & (key_at <= high[pl.ds(u + m, 1), cols])
                wt[p, half, cols] = jnp.where(keep, weights[half], 0.0).astype(BF16)
                sl[p, half, cols] = jnp.where(keep, slope[half], 0.0)
            att_t[:, cols] += dot(values_t, wt[p, :, cols])

    hand_on(0)

    def forward_step(i, _):
        hand_on(i)
        attend(i - 1)
        return 0

    lax.fori_loop(1, 8, forward_step, 0)
    attend(7)

    for k in range(4):
        block = att_t[:, k * T : (k + 1) * T]
        mean = jnp.sum(block, axis=0, keepdims=True) * (1.0 / DH)
        att_s[k, 0:T] = (block - mean).astype(BF16)
        high_part = mean.astype(BF16)
        rest = mean - high_part.astype(F32)
        mid_part = rest.astype(BF16)
        low_part = (rest - mid_part.astype(F32)).astype(BF16)
        r16 = lax.broadcasted_iota(jnp.int32, (16, T), 0)
        att_s[k, T : T + 16] = jnp.where(
            r16 == 0, high_part.astype(F32),
            jnp.where(r16 == 1, mid_part.astype(F32), jnp.where(r16 == 2, low_part.astype(F32), 0.0)),
        ).astype(BF16)
        push(att_s.at[k], ratt.at[hh], att_send.at[k], att_recv.at[hh], k)

    for i in range(1, 4):
        there = 2 * lax.rem(x + i, 4) + c
        arrived(dox.at[there], do_recv.at[there])
        remote(dox.at[there], dox.at[there], do_send.at[3 + i], do_recv.at[there], sib).start()

    for h in range(H):
        arrived(ratt.at[h], att_recv.at[h])
    rows = []
    for h in range(H):
        tail = jnp.sum(ratt[h, T : T + 16].astype(F32), axis=0, keepdims=True)
        rows.append(ratt[h, 0:T].astype(F32) + tail)
    mean = sum(jnp.sum(r, axis=0, keepdims=True) for r in rows) * (1.0 / 512)
    rows = [r - mean for r in rows]
    var = sum(jnp.sum(r * r, axis=0, keepdims=True) for r in rows) * (1.0 / 512)
    inv = lax.rsqrt(var + EPS)
    normed = [r * inv for r in rows]
    d_normed = []
    for h in range(H):
        feats = slice(h * DH, (h + 1) * DH)
        gates = gate_t[feats].astype(F32)
        d_gated = dgat[feats]
        gated_t[feats] = (normed[h] * gates).astype(BF16)
        gg_t[feats] = (d_gated * normed[h]).astype(BF16)
        d_normed.append(d_gated * gates)
    mean_d = sum(jnp.sum(d, axis=0, keepdims=True) for d in d_normed) * (1.0 / 512)
    mean_dn = sum(
        jnp.sum(d * n, axis=0, keepdims=True) for d, n in zip(d_normed, normed)
    ) * (1.0 / 512)
    for h in range(H):
        da_s[h] = ((d_normed[h] - mean_d - normed[h] * mean_dn) * inv).astype(BF16)
        push(da_s.at[h], rda.at[hh], da_send.at[h], da_recv.at[hh], h)

    for h in range(H):
        blocks = gated_t[h * DH : (h + 1) * DH].reshape(4, 2, 16, T)
        for cc in range(2):
            g_t[h, cc] = blocks[:, cc]
    g_to = [(x_dev(i, (c + cc) % 2 if cc == 0 else 1 - c), i, cc) for i in range(4) for cc in range(2)][1:]
    for n, (to, i, cc) in enumerate(g_to):
        core = c if cc == 0 else 1 - c
        remote(g_t.at[lax.rem(x + i, 4), core], gx.at[xc], g_send.at[n], g_recv.at[xc], to).start()
    gx[xc] = g_t[x, c]
    lo_v[...] = dot(gated_t[...], w_v[...], TN).astype(BF16)
    for h in range(H):
        feats = slice(h * DH, (h + 1) * DH)
        gg_v[:, feats] = gg_t[feats].T
    outs = [
        pltpu.make_async_copy(src, dst, out_sem.at[i])
        for i, (src, dst) in enumerate((
            (lo_v, lo_out.at[0]), (gg_v, gg_out.at[0]), (dq_v, dq_out.at[0]),
            (dk_v, dk_out.at[0]), (dv_v, dv_out.at[0]), (wa, wg_out),
        ))
    ]
    outs[0].start()
    outs[1].start()
    for i in range(4):
        theirs = 2 * lax.rem(x + i, 4) + 1 - c
        arrived(dox.at[theirs], do_recv.at[theirs])
        arrived(gx.at[theirs], g_recv.at[theirs])
        if i:
            arrived(gx.at[theirs + 2 * c - 1], g_recv.at[theirs + 2 * c - 1])
    for n in range(2):
        cols = slice(n * 512, (n + 1) * 512)
        part = dot(gx[0].reshape(64, T), dox[0, :, cols])
        for i in range(1, 8):
            part += dot(gx[i].reshape(64, T), dox[i, :, cols])
        wl_f[:, :, cols] = part.reshape(4, 16, 512)
        wl_s[:, :, cols] = part.astype(BF16).reshape(4, 16, 512)
    for i in range(1, 4):
        there = lax.rem(l + i, 4)
        remote(wl_s.at[there], wl_r.at[i - 1], l_send.at[i - 1], l_recv.at[i - 1], l_dev(i)).start()

    def piece(ref, s):
        down = pl.multiple_of(lax.div(s, 8) * 8, 8)
        across = pl.multiple_of(lax.rem(s, 8) * 128, 128)
        return ref.at[pl.ds(down, 8), pl.ds(across, 128)]

    def spread(i, _):
        there = lax.rem(sq + i, 16)
        remote(piece(ws, there), ws_r.at[i], s_send.at[i], s_recv.at[i], s_dev(i)).start()
        return 0

    for k in range(4):
        arrived(rda.at[k], da_recv.at[k])

    total = wl_f[l]
    for i in range(3):
        arrived(wl_r.at[i], l_recv.at[i])
        total += wl_r[i].astype(F32)
    ws[...] = total
    lax.fori_loop(1, 16, spread, 0)
    pltpu.make_async_copy(piece(ws, sq), ws_r.at[0], s_recv.at[0]).start()

    dq_t[...] = jnp.zeros_like(dq_t)

    def back(i):
        k, far = place(7 - i)
        p = 4 * far + k
        values = kv[p, 1]
        d_keys = jnp.zeros((2 * T, DH), F32)
        d_values = jnp.zeros((2 * T, DH), F32)
        for j in range(2):
            cols = slice(j * 256, (j + 1) * 256)
            grads_t = jnp.concatenate([rda[2 * j], rda[2 * j + 1]], axis=1)
            d_scores = (dot(values, grads_t) * sl[p, :, cols]).astype(BF16)
            d_keys += dot(d_scores, rq[2 * j : 2 * j + 2].reshape(256, DH))
            d_values += dot(wt[p, :, cols], grads_t, NT)
            dq_t[:, cols] += dot(kt[p], d_scores)
        dkv_f[i, 0] = d_keys
        dkv_f[i, 1] = d_values
        sib_s[i, 0] = dkv_f[i, 0, sib_rows].astype(BF16)
        sib_s[i, 1] = dkv_f[i, 1, sib_rows].astype(BF16)
        remote(sib_s.at[i], sib_r.at[i], sib_send.at[i], sib_recv.at[i], sib).start()

    def give(i):
        k, far = place(7 - i)
        arrived(sib_r.at[i], sib_recv.at[i])
        dkv_s[i, 0] = (dkv_f[i, 0, own_rows] + sib_r[i, 0].astype(F32)).astype(BF16)
        dkv_s[i, 1] = (dkv_f[i, 1, own_rows] + sib_r[i, 1].astype(F32)).astype(BF16)
        push(
            dkv_s.at[i], rdkv.at[far, hh], dkv_send.at[i], dkv_recv.at[4 * far + hh], k, far == 1
        )

    back(0)

    def back_step(i, _):
        back(i)
        give(i - 1)
        return 0

    lax.fori_loop(1, 8, back_step, 0)
    for k in range(4):
        dq_s[k] = dq_t[:, k * T : (k + 1) * T].T.astype(BF16)
        push(dq_s.at[k], rdq.at[hh], dq_send.at[k], dq_recv.at[hh], k)
    give(7)

    def fold(i, acc):
        arrived(ws_r.at[i], s_recv.at[i])
        return acc + ws_r[i]

    wa_s[...] = lax.fori_loop(0, 16, fold, jnp.zeros((8, 128), F32))

    def share(i, _):
        remote(wa_s, piece(wa, sq), a_send.at[i], a_recv.at[sq], s_dev(i)).start()
        return 0

    lax.fori_loop(1, 16, share, 0)
    pltpu.make_async_copy(wa_s, piece(wa, sq), a_recv.at[sq]).start()

    for h in range(H):
        cols = slice(h * DH, (h + 1) * DH)
        arrived(rdq.at[h], dq_recv.at[h])
        dq_v[:, cols] = rdq[h]
    outs[2].start()
    for h in range(H):
        cols = slice(h * DH, (h + 1) * DH)
        arrived(rdkv.at[0, h], dkv_recv.at[h])
        arrived(rdkv.at[1, h], dkv_recv.at[4 + h])
        dk_v[:, cols] = (rdkv[0, h, 0].astype(F32) + rdkv[1, h, 0].astype(F32)).astype(BF16)
        dv_v[:, cols] = (rdkv[0, h, 1].astype(F32) + rdkv[1, h, 1].astype(F32)).astype(BF16)

    outs[3].start()
    outs[4].start()

    def gathered(i, _):
        arrived(piece(wa, i), a_recv.at[i])
        return 0

    lax.fori_loop(0, 16, gathered, 0)
    outs[5].start()

    for k in range(4):
        pushed(q_s.at[k], rq.at[hh], q_send.at[k], q_recv.at[hh], k)
        pushed(att_s.at[k], ratt.at[hh], att_send.at[k], att_recv.at[hh], k)
        pushed(da_s.at[k], rda.at[hh], da_send.at[k], da_recv.at[hh], k)
        pushed(dq_s.at[k], rdq.at[hh], dq_send.at[k], dq_recv.at[hh], k)
        pushed(kv_s.at[k], kv.at[hh, :, my_rows], kv_send.at[k], kv_recv.at[y], k)
        remote(kv_s.at[k], kv.at[hh, :, my_rows], kv_send.at[4 + k], kv_recv.at[y], sib).wait_send()

    def left(i, _):
        here = kv.at[0, :, own_rows]
        remote(here, here, fwd_send.at[i], kv_recv.at[0], sib).wait_send()
        remote(sib_s.at[i], sib_r.at[i], sib_send.at[i], sib_recv.at[i], sib).wait_send()
        k, far = place(7 - i)
        pushed(dkv_s.at[i], rdkv.at[0, hh], dkv_send.at[i], dkv_recv.at[hh], k, far == 1)
        return 0

    lax.fori_loop(0, 8, left, 0)
    for i in range(7):
        remote(dox.at[0], dox.at[0], do_send.at[i], do_recv.at[0], sib).wait_send()
        remote(gx.at[0], gx.at[0], g_send.at[i], g_recv.at[0], sib).wait_send()
    for i in range(3):
        remote(wl_s.at[0], wl_r.at[i], l_send.at[i], l_recv.at[i], sib).wait_send()

    def left_seq(i, _):
        remote(wa_s, ws_r.at[i], s_send.at[i], s_recv.at[i], sib).wait_send()
        remote(wa_s, ws_r.at[i], a_send.at[i], a_recv.at[i], sib).wait_send()
        return 0

    lax.fori_loop(1, 16, left_seq, 0)
    for copy in outs:
        copy.wait()


def store(*refs):
    sem = refs[-1]
    copies = [pltpu.make_async_copy(refs[i], refs[6 + i], sem.at[i]) for i in range(6)]
    for copy in copies:
        copy.start()
    for copy in copies:
        copy.wait()


def body(queries, keys, values, gates, d_out, w_out, lengths, tile_owner, pattern):
    hbm = pl.BlockSpec(memory_space=pl.ANY)
    rows = jax.ShapeDtypeStruct((1, T, 512), BF16)
    outs = (
        jax.ShapeDtypeStruct((1, T, 1024), BF16), rows, rows, rows, rows,
        jax.ShapeDtypeStruct((16, 1024), F32),
    )
    dma = pltpu.SemaphoreType.DMA
    buf = pltpu.VMEM
    scratch = dict(
        lo_v=buf((T, 1024), BF16), dq_v=buf((T, 512), BF16), dk_v=buf((T, 512), BF16),
        dv_v=buf((T, 512), BF16), gg_v=buf((T, 512), BF16),
        kv_s=buf((4, 2, T, DH), BF16), q_s=buf((4, T, DH), BF16), g_v=buf((T, 512), BF16),
        w_v=buf((512, 1024), BF16), len_v=buf((1, 4), jnp.int32), own_v=buf((1, 16), jnp.int32),
        pat_v=buf((1, 16, 16), jnp.int32),
        meta_s=buf((24, 128), F32), meta_r=buf((24, 128), F32),
        kv=buf((8, 2, 2 * T, DH), BF16), rq=buf((4, T, DH), BF16), kt=buf((8, DH, 2 * T), BF16),
        wt=buf((8, 2 * T, 512), BF16), sl=buf((8, 2 * T, 512), F32),
        low=buf((16, 512), F32), high=buf((16, 512), F32),
        att_t=buf((DH, 512), F32), att_s=buf((4, T + 16, DH), BF16), ratt=buf((4, T + 16, DH), BF16),
        dgat=buf((512, T), F32), gate_t=buf((512, T), BF16), gated_t=buf((512, T), BF16),
        gg_t=buf((512, T), BF16),
        da_s=buf((4, T, DH), BF16), rda=buf((4, T, DH), BF16), dkv_f=buf((8, 2, 2 * T, DH), F32),
        sib_s=buf((8, 2, T, DH), BF16), sib_r=buf((8, 2, T, DH), BF16),
        dkv_s=buf((8, 2, T, DH), BF16), rdkv=buf((2, 4, 2, T, DH), BF16),
        dq_t=buf((DH, 512), F32), dq_s=buf((4, T, DH), BF16), rdq=buf((4, T, DH), BF16),
        dox=buf((8, T, 1024), BF16), g_t=buf((4, 2, 4, 16, T), BF16), gx=buf((8, 4, 16, T), BF16),
        wl_f=buf((4, 16, 1024), F32), wl_s=buf((4, 16, 1024), BF16), wl_r=buf((3, 16, 1024), BF16),
        ws=buf((16, 1024), F32), ws_r=buf((16, 8, 128), F32),
        wa_s=buf((8, 128), F32), wa=buf((16, 1024), F32),
        in_sem=dma((18,)), out_sem=dma((6,)), kv_send=dma((8,)), kv_recv=dma((16,)), fwd_send=dma((8,)),
        q_send=dma((4,)), q_recv=dma((4,)), meta_sem=dma((2,)), att_send=dma((4,)), att_recv=dma((4,)),
        da_send=dma((4,)), da_recv=dma((4,)), sib_send=dma((8,)), sib_recv=dma((8,)),
        dkv_send=dma((8,)), dkv_recv=dma((8,)), dq_send=dma((4,)), dq_recv=dma((4,)),
        do_send=dma((7,)), do_recv=dma((8,)), g_send=dma((7,)), g_recv=dma((8,)),
        l_send=dma((3,)), l_recv=dma((3,)),
        s_send=dma((16,)), s_recv=dma((16,)), a_send=dma((16,)), a_recv=dma((16,)),
    )
    results = pl.pallas_call(
        kernel,
        out_shape=outs,
        in_specs=[hbm] * 9,
        out_specs=(hbm,) * 6,
        scratch_shapes=list(scratch.values()),
        name="hstu",
        compiler_params=pltpu.CompilerParams(
            collective_id=0, has_side_effects=True, vmem_limit_bytes=VMEM
        ),
    )(queries, keys, values, gates, d_out, w_out, lengths, tile_owner, pattern)
    return pl.pallas_call(
        store,
        out_shape=outs,
        in_specs=[hbm] * 6,
        out_specs=(hbm,) * 6,
        scratch_shapes=[dma((6,))],
        name="store",
        compiler_params=pltpu.CompilerParams(vmem_limit_bytes=VMEM),
    )(*results)


def solution(mesh):
    rows = P("dp", "seq", None)
    in_specs = (rows, rows, rows, rows, rows, P(), P("dp", None), P("dp", None), P("dp", None, None))
    out_specs = (rows, rows, rows, rows, rows, P("dp", None))
    return jax.shard_map(body, mesh=mesh, in_specs=in_specs, out_specs=out_specs, check_vma=False)
```

```python
import jax
import jax.numpy as jnp
from jax import lax
from jax.experimental import pallas as pl
from jax.experimental.pallas import tpu as pltpu
from jax.sharding import PartitionSpec as P

H = 4
DH = 128
T = 128
F32 = jnp.float32
BF16 = jnp.bfloat16
MESH = pl.DeviceIdType.MESH
EPS = 1e-06
NT = (((1,), (1,)), ((), ()))
TN = (((0,), (0,)), ((), ()))
VMEM = 60 << 20
HALF_SCALE = 0.5 * DH ** (-0.5)


def dot(a, b, dims=(((1,), (0,)), ((), ()))):
    return lax.dot_general(a, b, dims, preferred_element_type=F32)


def kernel(
    q_ref, k_ref, v_ref, g_ref, do_ref, w_ref, len_ref, own_ref, pat_ref,
    lo_out, dq_out, dk_out, dv_out, gg_out, wg_out,
    lo_v, dq_v, dk_v, dv_v, gg_v, kv_s, q_s, g_v, w_v, len_v, own_v, pat_v,
    meta_s, meta_r, kv, rq, kt, wt, sl, low, high, att_t, att_s, ratt,
    dgat, gate_t, gated_t, gg_t, da_s, rda, dkv_f, sib_s, sib_r, dkv_s, rdkv, dq_t, dq_s, rdq,
    dox, g_t, gx, wl_f, wl_s, wl_r, ws, ws_r, wa_s, wa,
    in_sem, out_sem, kv_send, kv_recv, fwd_send, q_send, q_recv, meta_sem, att_send, att_recv,
    da_send, da_recv, sib_send, sib_recv, dkv_send, dkv_recv, dq_send, dq_recv,
    do_send, do_recv, g_send, g_recv, l_send, l_recv, s_send, s_recv, a_send, a_recv,
):
    dp = lax.axis_index("dp")
    sq = lax.axis_index("seq")
    x = lax.div(dp, 8)
    l = lax.rem(lax.div(dp, 2), 4)
    c = lax.rem(dp, 2)
    y = lax.div(sq, 2)
    z = lax.rem(sq, 2)
    par = lax.rem(y, 2)
    hh = lax.div(y, 2)
    xc = x * 2 + c
    sib = (dp + 1 - 2 * c, sq)
    own_par = par == c
    own_rows = pl.ds(pl.multiple_of(c * T, T), T)
    sib_rows = pl.ds(pl.multiple_of((1 - c) * T, T), T)
    my_rows = pl.ds(pl.multiple_of(par * T, T), T)

    def partner(k, far):
        return (dp - c + par, (2 * k + c) * 2 + jnp.where(far, 1 - z, z))

    def is_self(k, far):
        return own_par & (k == hh) & jnp.logical_not(far)

    def remote(src, dst, send, recv, to):
        return pltpu.make_async_remote_copy(
            src_ref=src, dst_ref=dst, send_sem=send, recv_sem=recv, device_id=to,
            device_id_type=MESH,
        )

    def arrived(dst, sem):
        pltpu.make_async_copy(dst, dst, sem).wait()

    def push(src, dst, send, recv, k, far=False):
        if far is True:
            remote(src, dst, send, recv, partner(k, far)).start()
            return
        me = is_self(k, far)

        @pl.when(jnp.logical_not(me))
        def _():
            remote(src, dst, send, recv, partner(k, far)).start()

        @pl.when(me)
        def _():
            pltpu.make_async_copy(src, dst, recv).start()

    def pushed(src, dst, send, recv, k, far=False):
        @pl.when(jnp.logical_not(is_self(k, far)))
        def _():
            remote(src, dst, send, recv, partner(k, far)).wait_send()

    def x_dev(i, cc):
        return (lax.rem(x + i, 4) * 8 + l * 2 + cc, sq)

    def l_dev(i):
        return (x * 8 + lax.rem(l + i, 4) * 2 + c, sq)

    def s_dev(i):
        return (dp, lax.rem(sq + i, 16))

    loads = []

    def load(src, dst):
        copy = pltpu.make_async_copy(src, dst, in_sem.at[len(loads)])
        copy.start()
        loads.append(copy)

    load(len_ref, len_v)
    load(own_ref, own_v)
    load(pat_ref, pat_v)
    for h in range(H):
        cols = pl.ds(h * DH, DH)
        load(q_ref.at[0, :, cols], q_s.at[h])
        load(k_ref.at[0, :, cols], kv_s.at[h, 0])
        load(v_ref.at[0, :, cols], kv_s.at[h, 1])
    load(do_ref.at[0], dox.at[xc])
    load(w_ref, w_v)
    load(g_ref.at[0], g_v)

    barrier = pltpu.get_barrier_semaphore()

    def tell(to):
        pl.semaphore_signal(barrier, inc=1, device_id=to, device_id_type=MESH)

    for k in range(4):
        tell(partner(k, True))
        @pl.when(jnp.logical_not(is_self(k, False)))
        def _():
            tell(partner(k, False))
    tell(sib)
    for i in range(1, 4):
        tell(x_dev(i, c))
        tell(x_dev(i, 1 - c))
        tell(l_dev(i))
    for i in range(1, 16):
        tell(s_dev(i))

    for copy in loads[:3]:
        copy.wait()
    meta_s[...] = jnp.zeros_like(meta_s)
    meta_s[0:1, 0:4] = len_v[...].astype(F32)
    meta_s[1:2, 0:16] = own_v[...].astype(F32)
    meta_s[8:24, 0:16] = pat_v[0].astype(F32)
    for copy in loads[3:15]:
        copy.wait()

    pl.semaphore_wait(barrier, 33 - jnp.where(own_par, 1, 0))

    meta_copy = remote(meta_s, meta_r, meta_sem.at[0], meta_sem.at[1], sib)
    meta_copy.start()
    for k in range(4):
        push(q_s.at[k], rq.at[hh], q_send.at[k], q_recv.at[hh], k)
    for k in range(4):
        push(kv_s.at[k], kv.at[4 + hh, :, my_rows], kv_send.at[4 + k], kv_recv.at[8 + y], k, True)
        push(kv_s.at[k], kv.at[hh, :, my_rows], kv_send.at[k], kv_recv.at[y], k)
    for copy in loads[15:]:
        copy.wait()
    remote(dox.at[xc], dox.at[xc], do_send.at[0], do_recv.at[xc], sib).start()
    for i in range(1, 4):
        remote(dox.at[xc], dox.at[xc], do_send.at[i], do_recv.at[xc], x_dev(i, c)).start()

    def place(i):
        step = lax.rem(i, 4)
        turn = jnp.where(step == 2, 3, jnp.where(step == 3, 2, step))
        return lax.rem(hh + turn, 4), lax.div(i, 4)

    dgat[...] = dot(w_v[...], dox[xc], NT)
    for h in range(H):
        gate_t[h * DH : (h + 1) * DH] = g_v[:, h * DH : (h + 1) * DH].T

    meta_copy.wait()
    meta = jnp.where(own_par, meta_s[...], meta_r[...])
    lane = lax.broadcasted_iota(jnp.int32, (16, 128), 1).astype(F32)
    slot = lax.broadcasted_iota(jnp.int32, (16, 128), 0)
    seat = (2 * lax.rem(slot, 8) + jnp.where(slot < 8, z, 1 - z)).astype(F32)
    hot = jnp.where((meta[1:2] == seat) & (lane < 16), 1.0, 0.0)
    tile = jnp.sum(hot * lane, axis=1, keepdims=True)
    col = lax.broadcasted_iota(jnp.int32, (16, 512), 1)
    row = lax.broadcasted_iota(jnp.int32, (16, 512), 0)
    query_hot = jnp.where(row == 2 * lax.div(col, 128) + c, 1.0, 0.0)
    query_tile = jnp.sum(tile * query_hot, axis=0, keepdims=True)
    pos = query_tile * T + lax.rem(col, 128)[0:1].astype(F32)
    upto = slot[0:8].astype(F32)
    lengths = jnp.where((lane[0:8] <= upto) & (lane[0:8] < 4), meta[0:1], 0.0)
    ends = jnp.sum(lengths, axis=1, keepdims=True)
    first = jnp.max(jnp.where(ends <= pos, ends, 0.0), axis=0, keepdims=True)
    tile_hot = jnp.where(row.astype(F32) == query_tile, 1.0, 0.0)
    seen = dot(meta[8:24], tile_hot, TN)
    allow = (dot(hot, seen) > 0.5) | (tile == query_tile)
    low[...] = jnp.where(allow, first - tile * T, 1e6)
    high[...] = pos - tile * T

    for k in range(4):
        arrived(rq.at[k], q_recv.at[k])

    att_t[...] = jnp.zeros_like(att_t)

    def hand_on(i):
        k, far = place(i)
        here = kv.at[4 * far + k, :, own_rows]
        u = 8 * far + 2 * k + c
        arrived(here, kv_recv.at[u])
        remote(here, here, fwd_send.at[i], kv_recv.at[u], sib).start()

    def attend(i):
        k, far = place(i)
        p = 4 * far + k
        u = 8 * far + 2 * k
        arrived(kv.at[p, :, sib_rows], kv_recv.at[u + 1 - c])
        keys = kv[p, 0]
        values_t = kv[p, 1].T
        kt[p] = keys.T
        key_at = lax.broadcasted_iota(jnp.int32, (T, 256), 0).astype(F32)
        for j in range(2):
            cols = slice(j * 256, (j + 1) * 256)
            part = dot(keys, rq[2 * j : 2 * j + 2].reshape(256, DH), NT) * HALF_SCALE
            tan = jnp.tanh(part)
            weights = part + part * tan
            sl[p, :, cols] = part
            for m in range(2):
                half = slice(m * T, (m + 1) * T)
                keep = (key_at >= low[pl.ds(u + m, 1), cols]) & (key_at <= high[pl.ds(u + m, 1), cols])
                wt[p, half, cols] = jnp.where(keep, weights[half], 0.0).astype(BF16)
            att_t[:, cols] += dot(values_t, wt[p, :, cols])

    hand_on(0)

    def forward_step(i, _):
        hand_on(i)
        attend(i - 1)
        return 0

    lax.fori_loop(1, 8, forward_step, 0)
    attend(7)

    for k in range(4):
        block = att_t[:, k * T : (k + 1) * T]
        mean = jnp.sum(block, axis=0, keepdims=True) * (1.0 / DH)
        att_s[k, 0:T] = (block - mean).astype(BF16)
        high_part = mean.astype(BF16)
        rest = mean - high_part.astype(F32)
        mid_part = rest.astype(BF16)
        low_part = (rest - mid_part.astype(F32)).astype(BF16)
        r16 = lax.broadcasted_iota(jnp.int32, (16, T), 0)
        att_s[k, T : T + 16] = jnp.where(
            r16 == 0, high_part.astype(F32),
            jnp.where(r16 == 1, mid_part.astype(F32), jnp.where(r16 == 2, low_part.astype(F32), 0.0)),
        ).astype(BF16)
        push(att_s.at[k], ratt.at[hh], att_send.at[k], att_recv.at[hh], k)

    for i in range(1, 4):
        there = 2 * lax.rem(x + i, 4) + c
        arrived(dox.at[there], do_recv.at[there])
        remote(dox.at[there], dox.at[there], do_send.at[3 + i], do_recv.at[there], sib).start()

    def slopes(p, _):
        u = 8 * lax.div(p, 4) + 2 * lax.rem(p, 4)
        key_at = lax.broadcasted_iota(jnp.int32, (T, 256), 0).astype(F32)
        for j in range(2):
            cols = slice(j * 256, (j + 1) * 256)
            for m in range(2):
                half = slice(m * T, (m + 1) * T)
                part = sl[p, half, cols]
                tan = jnp.tanh(part)
                slope = (1.0 + tan) * (HALF_SCALE + (part * HALF_SCALE) * (1.0 - tan))
                keep = (key_at >= low[pl.ds(u + m, 1), cols]) & (key_at <= high[pl.ds(u + m, 1), cols])
                sl[p, half, cols] = jnp.where(keep, slope, 0.0)
        return 0

    lax.fori_loop(0, 8, slopes, 0)

    for h in range(H):
        arrived(ratt.at[h], att_recv.at[h])
    rows = []
    for h in range(H):
        tail = jnp.sum(ratt[h, T : T + 16].astype(F32), axis=0, keepdims=True)
        rows.append(ratt[h, 0:T].astype(F32) + tail)
    mean = sum(jnp.sum(r, axis=0, keepdims=True) for r in rows) * (1.0 / 512)
    rows = [r - mean for r in rows]
    var = sum(jnp.sum(r * r, axis=0, keepdims=True) for r in rows) * (1.0 / 512)
    inv = lax.rsqrt(var + EPS)
    normed = [r * inv for r in rows]
    d_normed = []
    for h in range(H):
        feats = slice(h * DH, (h + 1) * DH)
        gates = gate_t[feats].astype(F32)
        d_gated = dgat[feats]
        gated_t[feats] = (normed[h] * gates).astype(BF16)
        gg_t[feats] = (d_gated * normed[h]).astype(BF16)
        d_normed.append(d_gated * gates)
    mean_d = sum(jnp.sum(d, axis=0, keepdims=True) for d in d_normed) * (1.0 / 512)
    mean_dn = sum(
        jnp.sum(d * n, axis=0, keepdims=True) for d, n in zip(d_normed, normed)
    ) * (1.0 / 512)
    for h in range(H):
        da_s[h] = ((d_normed[h] - mean_d - normed[h] * mean_dn) * inv).astype(BF16)
        push(da_s.at[h], rda.at[hh], da_send.at[h], da_recv.at[hh], h)

    for h in range(H):
        blocks = gated_t[h * DH : (h + 1) * DH].reshape(4, 2, 16, T)
        for cc in range(2):
            g_t[h, cc] = blocks[:, cc]
    g_to = [(x_dev(i, (c + cc) % 2 if cc == 0 else 1 - c), i, cc) for i in range(4) for cc in range(2)][1:]
    for n, (to, i, cc) in enumerate(g_to):
        core = c if cc == 0 else 1 - c
        remote(g_t.at[lax.rem(x + i, 4), core], gx.at[xc], g_send.at[n], g_recv.at[xc], to).start()
    gx[xc] = g_t[x, c]
    lo_v[...] = dot(gated_t[...], w_v[...], TN).astype(BF16)
    for h in range(H):
        feats = slice(h * DH, (h + 1) * DH)
        gg_v[:, feats] = gg_t[feats].T
    outs = [
        pltpu.make_async_copy(src, dst, out_sem.at[i])
        for i, (src, dst) in enumerate((
            (lo_v, lo_out.at[0]), (gg_v, gg_out.at[0]), (dq_v, dq_out.at[0]),
            (dk_v, dk_out.at[0]), (dv_v, dv_out.at[0]), (wa, wg_out),
        ))
    ]
    outs[0].start()
    outs[1].start()
    for i in range(4):
        theirs = 2 * lax.rem(x + i, 4) + 1 - c
        arrived(dox.at[theirs], do_recv.at[theirs])
        arrived(gx.at[theirs], g_recv.at[theirs])
        if i:
            arrived(gx.at[theirs + 2 * c - 1], g_recv.at[theirs + 2 * c - 1])
    for n in range(2):
        cols = slice(n * 512, (n + 1) * 512)
        part = dot(gx[0].reshape(64, T), dox[0, :, cols])
        for i in range(1, 8):
            part += dot(gx[i].reshape(64, T), dox[i, :, cols])
        wl_f[:, :, cols] = part.reshape(4, 16, 512)
        wl_s[:, :, cols] = part.astype(BF16).reshape(4, 16, 512)
    for i in range(1, 4):
        there = lax.rem(l + i, 4)
        remote(wl_s.at[there], wl_r.at[i - 1], l_send.at[i - 1], l_recv.at[i - 1], l_dev(i)).start()

    def piece(ref, s):
        down = pl.multiple_of(lax.div(s, 8) * 8, 8)
        across = pl.multiple_of(lax.rem(s, 8) * 128, 128)
        return ref.at[pl.ds(down, 8), pl.ds(across, 128)]

    def spread(i, _):
        there = lax.rem(sq + i, 16)
        remote(piece(ws, there), ws_r.at[i], s_send.at[i], s_recv.at[i], s_dev(i)).start()
        return 0

    for k in range(4):
        arrived(rda.at[k], da_recv.at[k])

    dq_t[...] = jnp.zeros_like(dq_t)

    def back(i):
        k, far = place(7 - i)
        p = 4 * far + k
        values = kv[p, 1]
        d_keys = jnp.zeros((2 * T, DH), F32)
        d_values = jnp.zeros((2 * T, DH), F32)
        for j in range(2):
            cols = slice(j * 256, (j + 1) * 256)
            grads_t = jnp.concatenate([rda[2 * j], rda[2 * j + 1]], axis=1)
            d_scores = (dot(values, grads_t) * sl[p, :, cols]).astype(BF16)
            d_keys += dot(d_scores, rq[2 * j : 2 * j + 2].reshape(256, DH))
            d_values += dot(wt[p, :, cols], grads_t, NT)
            dq_t[:, cols] += dot(kt[p], d_scores)
        dkv_f[i, 0] = d_keys
        dkv_f[i, 1] = d_values
        sib_s[i, 0] = dkv_f[i, 0, sib_rows].astype(BF16)
        sib_s[i, 1] = dkv_f[i, 1, sib_rows].astype(BF16)
        remote(sib_s.at[i], sib_r.at[i], sib_send.at[i], sib_recv.at[i], sib).start()

    def give(i):
        k, far = place(7 - i)
        arrived(sib_r.at[i], sib_recv.at[i])
        dkv_s[i, 0] = (dkv_f[i, 0, own_rows] + sib_r[i, 0].astype(F32)).astype(BF16)
        dkv_s[i, 1] = (dkv_f[i, 1, own_rows] + sib_r[i, 1].astype(F32)).astype(BF16)
        push(
            dkv_s.at[i], rdkv.at[far, hh], dkv_send.at[i], dkv_recv.at[4 * far + hh], k, far == 1
        )

    back(0)

    def back_step(i, _):
        back(i)
        give(i - 1)
        return 0

    lax.fori_loop(1, 8, back_step, 0)
    for k in range(4):
        dq_s[k] = dq_t[:, k * T : (k + 1) * T].T.astype(BF16)
        push(dq_s.at[k], rdq.at[hh], dq_send.at[k], dq_recv.at[hh], k)
    give(7)

    total = wl_f[l]
    for i in range(3):
        arrived(wl_r.at[i], l_recv.at[i])
        total += wl_r[i].astype(F32)
    ws[...] = total
    lax.fori_loop(1, 16, spread, 0)
    pltpu.make_async_copy(piece(ws, sq), ws_r.at[0], s_recv.at[0]).start()

    def fold(i, acc):
        arrived(ws_r.at[i], s_recv.at[i])
        return acc + ws_r[i]

    wa_s[...] = lax.fori_loop(0, 16, fold, jnp.zeros((8, 128), F32))

    def share(i, _):
        remote(wa_s, piece(wa, sq), a_send.at[i], a_recv.at[sq], s_dev(i)).start()
        return 0

    lax.fori_loop(1, 16, share, 0)
    pltpu.make_async_copy(wa_s, piece(wa, sq), a_recv.at[sq]).start()

    for h in range(H):
        cols = slice(h * DH, (h + 1) * DH)
        arrived(rdq.at[h], dq_recv.at[h])
        dq_v[:, cols] = rdq[h]
    outs[2].start()
    for h in range(H):
        cols = slice(h * DH, (h + 1) * DH)
        arrived(rdkv.at[0, h], dkv_recv.at[h])
        arrived(rdkv.at[1, h], dkv_recv.at[4 + h])
        dk_v[:, cols] = (rdkv[0, h, 0].astype(F32) + rdkv[1, h, 0].astype(F32)).astype(BF16)
        dv_v[:, cols] = (rdkv[0, h, 1].astype(F32) + rdkv[1, h, 1].astype(F32)).astype(BF16)

    outs[3].start()
    outs[4].start()

    def gathered(i, _):
        arrived(piece(wa, i), a_recv.at[i])
        return 0

    lax.fori_loop(0, 16, gathered, 0)
    outs[5].start()

    for k in range(4):
        pushed(q_s.at[k], rq.at[hh], q_send.at[k], q_recv.at[hh], k)
        pushed(att_s.at[k], ratt.at[hh], att_send.at[k], att_recv.at[hh], k)
        pushed(da_s.at[k], rda.at[hh], da_send.at[k], da_recv.at[hh], k)
        pushed(dq_s.at[k], rdq.at[hh], dq_send.at[k], dq_recv.at[hh], k)
        pushed(kv_s.at[k], kv.at[hh, :, my_rows], kv_send.at[k], kv_recv.at[y], k)
        remote(kv_s.at[k], kv.at[hh, :, my_rows], kv_send.at[4 + k], kv_recv.at[y], sib).wait_send()

    def left(i, _):
        here = kv.at[0, :, own_rows]
        remote(here, here, fwd_send.at[i], kv_recv.at[0], sib).wait_send()
        remote(sib_s.at[i], sib_r.at[i], sib_send.at[i], sib_recv.at[i], sib).wait_send()
        k, far = place(7 - i)
        pushed(dkv_s.at[i], rdkv.at[0, hh], dkv_send.at[i], dkv_recv.at[hh], k, far == 1)
        return 0

    lax.fori_loop(0, 8, left, 0)
    for i in range(7):
        remote(dox.at[0], dox.at[0], do_send.at[i], do_recv.at[0], sib).wait_send()
        remote(gx.at[0], gx.at[0], g_send.at[i], g_recv.at[0], sib).wait_send()
    for i in range(3):
        remote(wl_s.at[0], wl_r.at[i], l_send.at[i], l_recv.at[i], sib).wait_send()

    def left_seq(i, _):
        remote(wa_s, ws_r.at[i], s_send.at[i], s_recv.at[i], sib).wait_send()
        remote(wa_s, ws_r.at[i], a_send.at[i], a_recv.at[i], sib).wait_send()
        return 0

    lax.fori_loop(1, 16, left_seq, 0)
    for copy in outs:
        copy.wait()


def store(*refs):
    ins, outs, held, sem = refs[:6], refs[6:12], refs[12:18], refs[18]
    loads = [pltpu.make_async_copy(ins[i], held[i], sem.at[0, i]) for i in range(6)]
    stores = [pltpu.make_async_copy(held[i], outs[i], sem.at[1, i]) for i in range(6)]
    for copy in loads:
        copy.start()
    for i in range(6):
        loads[i].wait()
        stores[i].start()
    for copy in stores:
        copy.wait()


def body(queries, keys, values, gates, d_out, w_out, lengths, tile_owner, pattern):
    hbm = pl.BlockSpec(memory_space=pl.ANY)
    rows = jax.ShapeDtypeStruct((1, T, 512), BF16)
    outs = (
        jax.ShapeDtypeStruct((1, T, 1024), BF16), rows, rows, rows, rows,
        jax.ShapeDtypeStruct((16, 1024), F32),
    )
    dma = pltpu.SemaphoreType.DMA
    buf = pltpu.VMEM
    scratch = dict(
        lo_v=buf((T, 1024), BF16), dq_v=buf((T, 512), BF16), dk_v=buf((T, 512), BF16),
        dv_v=buf((T, 512), BF16), gg_v=buf((T, 512), BF16),
        kv_s=buf((4, 2, T, DH), BF16), q_s=buf((4, T, DH), BF16), g_v=buf((T, 512), BF16),
        w_v=buf((512, 1024), BF16), len_v=buf((1, 4), jnp.int32), own_v=buf((1, 16), jnp.int32),
        pat_v=buf((1, 16, 16), jnp.int32),
        meta_s=buf((24, 128), F32), meta_r=buf((24, 128), F32),
        kv=buf((8, 2, 2 * T, DH), BF16), rq=buf((4, T, DH), BF16), kt=buf((8, DH, 2 * T), BF16),
        wt=buf((8, 2 * T, 512), BF16), sl=buf((8, 2 * T, 512), F32),
        low=buf((16, 512), F32), high=buf((16, 512), F32),
        att_t=buf((DH, 512), F32), att_s=buf((4, T + 16, DH), BF16), ratt=buf((4, T + 16, DH), BF16),
        dgat=buf((512, T), F32), gate_t=buf((512, T), BF16), gated_t=buf((512, T), BF16),
        gg_t=buf((512, T), BF16),
        da_s=buf((4, T, DH), BF16), rda=buf((4, T, DH), BF16), dkv_f=buf((8, 2, 2 * T, DH), F32),
        sib_s=buf((8, 2, T, DH), BF16), sib_r=buf((8, 2, T, DH), BF16),
        dkv_s=buf((8, 2, T, DH), BF16), rdkv=buf((2, 4, 2, T, DH), BF16),
        dq_t=buf((DH, 512), F32), dq_s=buf((4, T, DH), BF16), rdq=buf((4, T, DH), BF16),
        dox=buf((8, T, 1024), BF16), g_t=buf((4, 2, 4, 16, T), BF16), gx=buf((8, 4, 16, T), BF16),
        wl_f=buf((4, 16, 1024), F32), wl_s=buf((4, 16, 1024), BF16), wl_r=buf((3, 16, 1024), BF16),
        ws=buf((16, 1024), F32), ws_r=buf((16, 8, 128), F32),
        wa_s=buf((8, 128), F32), wa=buf((16, 1024), F32),
        in_sem=dma((18,)), out_sem=dma((6,)), kv_send=dma((8,)), kv_recv=dma((16,)), fwd_send=dma((8,)),
        q_send=dma((4,)), q_recv=dma((4,)), meta_sem=dma((2,)), att_send=dma((4,)), att_recv=dma((4,)),
        da_send=dma((4,)), da_recv=dma((4,)), sib_send=dma((8,)), sib_recv=dma((8,)),
        dkv_send=dma((8,)), dkv_recv=dma((8,)), dq_send=dma((4,)), dq_recv=dma((4,)),
        do_send=dma((7,)), do_recv=dma((8,)), g_send=dma((7,)), g_recv=dma((8,)),
        l_send=dma((3,)), l_recv=dma((3,)),
        s_send=dma((16,)), s_recv=dma((16,)), a_send=dma((16,)), a_recv=dma((16,)),
    )
    results = pl.pallas_call(
        kernel,
        out_shape=outs,
        in_specs=[hbm] * 9,
        out_specs=(hbm,) * 6,
        scratch_shapes=list(scratch.values()),
        name="hstu",
        compiler_params=pltpu.CompilerParams(
            collective_id=0, has_side_effects=True, vmem_limit_bytes=VMEM
        ),
    )(queries, keys, values, gates, d_out, w_out, lengths, tile_owner, pattern)
    return pl.pallas_call(
        store,
        out_shape=outs,
        in_specs=[hbm] * 6,
        out_specs=(hbm,) * 6,
        scratch_shapes=[buf(o.shape, o.dtype) for o in outs] + [dma((2, 6))],
        name="store",
        compiler_params=pltpu.CompilerParams(vmem_limit_bytes=VMEM),
    )(*results)


def solution(mesh):
    rows = P("dp", "seq", None)
    in_specs = (rows, rows, rows, rows, rows, P(), P("dp", None), P("dp", None), P("dp", None, None))
    out_specs = (rows, rows, rows, rows, rows, P("dp", None))
    return jax.shard_map(body, mesh=mesh, in_specs=in_specs, out_specs=out_specs, check_vma=False)
```

```python
import jax
import jax.numpy as jnp
from jax import lax
from jax.experimental import pallas as pl
from jax.experimental.pallas import tpu as pltpu
from jax.sharding import PartitionSpec as P

H = 4
DH = 128
T = 128
F32 = jnp.float32
BF16 = jnp.bfloat16
MESH = pl.DeviceIdType.MESH
EPS = 1e-06
NT = (((1,), (1,)), ((), ()))
TN = (((0,), (0,)), ((), ()))
VMEM = 60 << 20
HALF_SCALE = 0.5 * DH ** (-0.5)


def dot(a, b, dims=(((1,), (0,)), ((), ()))):
    return lax.dot_general(a, b, dims, preferred_element_type=F32)


def kernel(
    q_ref, k_ref, v_ref, g_ref, do_ref, w_ref, len_ref, own_ref, pat_ref,
    lo_out, dq_out, dk_out, dv_out, gg_out, wg_out,
    lo_v, dq_v, dk_v, dv_v, gg_v, kv_s, q_s, g_v, w_v, len_v, own_v, pat_v,
    meta_s, meta_r, kv, rq, kt, wt, sl, low, high, att_t, att_s, ratt,
    dgat, gate_t, gated_t, gg_t, da_s, rda, dkv_f, sib_s, sib_r, dkv_s, rdkv, dq_t, dq_s, rdq,
    dox, g_t, gx, wl_f, wl_s, wl_r, near, far_w, wa,
    in_sem, out_sem, kv_send, kv_recv, fwd_send, q_send, q_recv, meta_sem, att_send, att_recv,
    da_send, da_recv, sib_send, sib_recv, dkv_send, dkv_recv, dq_send, dq_recv,
    do_send, do_recv, g_send, g_recv, l_send, l_recv, n_send, n_recv, f_send, f_recv,
):
    dp = lax.axis_index("dp")
    sq = lax.axis_index("seq")
    x = lax.div(dp, 8)
    l = lax.rem(lax.div(dp, 2), 4)
    c = lax.rem(dp, 2)
    y = lax.div(sq, 2)
    z = lax.rem(sq, 2)
    par = lax.rem(y, 2)
    hh = lax.div(y, 2)
    xc = x * 2 + c
    sib = (dp + 1 - 2 * c, sq)
    own_par = par == c
    own_rows = pl.ds(pl.multiple_of(c * T, T), T)
    sib_rows = pl.ds(pl.multiple_of((1 - c) * T, T), T)
    my_rows = pl.ds(pl.multiple_of(par * T, T), T)

    def partner(k, far):
        return (dp - c + par, (2 * k + c) * 2 + jnp.where(far, 1 - z, z))

    def is_self(k, far):
        return own_par & (k == hh) & jnp.logical_not(far)

    def remote(src, dst, send, recv, to):
        return pltpu.make_async_remote_copy(
            src_ref=src, dst_ref=dst, send_sem=send, recv_sem=recv, device_id=to,
            device_id_type=MESH,
        )

    def arrived(dst, sem):
        pltpu.make_async_copy(dst, dst, sem).wait()

    def push(src, dst, send, recv, k, far=False):
        if far is True:
            remote(src, dst, send, recv, partner(k, far)).start()
            return
        me = is_self(k, far)

        @pl.when(jnp.logical_not(me))
        def _():
            remote(src, dst, send, recv, partner(k, far)).start()

        @pl.when(me)
        def _():
            pltpu.make_async_copy(src, dst, recv).start()

    def pushed(src, dst, send, recv, k, far=False):
        @pl.when(jnp.logical_not(is_self(k, far)))
        def _():
            remote(src, dst, send, recv, partner(k, far)).wait_send()

    def x_dev(i, cc):
        return (lax.rem(x + i, 4) * 8 + l * 2 + cc, sq)

    def l_dev(i):
        return (x * 8 + lax.rem(l + i, 4) * 2 + c, sq)

    def near_dev(i):
        return (dp, (lax.div(y, 4) * 4 + lax.rem(y + i, 4)) * 2 + z)

    def far_dev(i):
        there = lax.rem(lax.div(y, 4) * 2 + z + i, 4)
        return (dp, (lax.div(there, 2) * 4 + lax.rem(y, 4)) * 2 + lax.rem(there, 2))

    loads = []

    def load(src, dst):
        copy = pltpu.make_async_copy(src, dst, in_sem.at[len(loads)])
        copy.start()
        loads.append(copy)

    load(len_ref, len_v)
    load(own_ref, own_v)
    load(pat_ref, pat_v)
    for h in range(H):
        cols = pl.ds(h * DH, DH)
        load(q_ref.at[0, :, cols], q_s.at[h])
        load(k_ref.at[0, :, cols], kv_s.at[h, 0])
        load(v_ref.at[0, :, cols], kv_s.at[h, 1])
    load(do_ref.at[0], dox.at[xc])
    load(w_ref, w_v)
    load(g_ref.at[0], g_v)

    barrier = pltpu.get_barrier_semaphore()

    def tell(to):
        pl.semaphore_signal(barrier, inc=1, device_id=to, device_id_type=MESH)

    for k in range(4):
        tell(partner(k, True))
        @pl.when(jnp.logical_not(is_self(k, False)))
        def _():
            tell(partner(k, False))
    tell(sib)
    for i in range(1, 4):
        tell(x_dev(i, c))
        tell(x_dev(i, 1 - c))
        tell(l_dev(i))
        tell(near_dev(i))
        tell(far_dev(i))

    for copy in loads[:3]:
        copy.wait()
    meta_s[...] = jnp.zeros_like(meta_s)
    meta_s[0:1, 0:4] = len_v[...].astype(F32)
    meta_s[1:2, 0:16] = own_v[...].astype(F32)
    meta_s[8:24, 0:16] = pat_v[0].astype(F32)
    for copy in loads[3:15]:
        copy.wait()

    pl.semaphore_wait(barrier, 24 - jnp.where(own_par, 1, 0))

    meta_copy = remote(meta_s, meta_r, meta_sem.at[0], meta_sem.at[1], sib)
    meta_copy.start()
    for k in range(4):
        push(q_s.at[k], rq.at[hh], q_send.at[k], q_recv.at[hh], k)
    for k in range(4):
        push(kv_s.at[k], kv.at[4 + hh, :, my_rows], kv_send.at[4 + k], kv_recv.at[8 + y], k, True)
        push(kv_s.at[k], kv.at[hh, :, my_rows], kv_send.at[k], kv_recv.at[y], k)
    for copy in loads[15:]:
        copy.wait()
    remote(dox.at[xc], dox.at[xc], do_send.at[0], do_recv.at[xc], sib).start()
    for i in range(1, 4):
        remote(dox.at[xc], dox.at[xc], do_send.at[i], do_recv.at[xc], x_dev(i, c)).start()

    def place(i):
        step = lax.rem(i, 4)
        turn = jnp.where(step == 2, 3, jnp.where(step == 3, 2, step))
        return lax.rem(hh + turn, 4), lax.div(i, 4)

    dgat[...] = dot(w_v[...], dox[xc], NT)
    for h in range(H):
        gate_t[h * DH : (h + 1) * DH] = g_v[:, h * DH : (h + 1) * DH].T

    meta_copy.wait()
    meta = jnp.where(own_par, meta_s[...], meta_r[...])
    lane = lax.broadcasted_iota(jnp.int32, (16, 128), 1).astype(F32)
    slot = lax.broadcasted_iota(jnp.int32, (16, 128), 0)
    seat = (2 * lax.rem(slot, 8) + jnp.where(slot < 8, z, 1 - z)).astype(F32)
    hot = jnp.where((meta[1:2] == seat) & (lane < 16), 1.0, 0.0)
    tile = jnp.sum(hot * lane, axis=1, keepdims=True)
    col = lax.broadcasted_iota(jnp.int32, (16, 512), 1)
    row = lax.broadcasted_iota(jnp.int32, (16, 512), 0)
    query_hot = jnp.where(row == 2 * lax.div(col, 128) + c, 1.0, 0.0)
    query_tile = jnp.sum(tile * query_hot, axis=0, keepdims=True)
    pos = query_tile * T + lax.rem(col, 128)[0:1].astype(F32)
    upto = slot[0:8].astype(F32)
    lengths = jnp.where((lane[0:8] <= upto) & (lane[0:8] < 4), meta[0:1], 0.0)
    ends = jnp.sum(lengths, axis=1, keepdims=True)
    first = jnp.max(jnp.where(ends <= pos, ends, 0.0), axis=0, keepdims=True)
    tile_hot = jnp.where(row.astype(F32) == query_tile, 1.0, 0.0)
    seen = dot(meta[8:24], tile_hot, TN)
    allow = (dot(hot, seen) > 0.5) | (tile == query_tile)
    low[...] = jnp.where(allow, first - tile * T, 1e6)
    high[...] = pos - tile * T

    for k in range(4):
        arrived(rq.at[k], q_recv.at[k])

    att_t[...] = jnp.zeros_like(att_t)

    def hand_on(i):
        k, far = place(i)
        here = kv.at[4 * far + k, :, own_rows]
        u = 8 * far + 2 * k + c
        arrived(here, kv_recv.at[u])
        remote(here, here, fwd_send.at[i], kv_recv.at[u], sib).start()

    def attend(i):
        k, far = place(i)
        p = 4 * far + k
        u = 8 * far + 2 * k
        arrived(kv.at[p, :, sib_rows], kv_recv.at[u + 1 - c])
        keys = kv[p, 0]
        values_t = kv[p, 1].T
        kt[p] = keys.T
        key_at = lax.broadcasted_iota(jnp.int32, (T, 256), 0).astype(F32)
        for j in range(2):
            cols = slice(j * 256, (j + 1) * 256)
            part = dot(keys, rq[2 * j : 2 * j + 2].reshape(256, DH), NT) * HALF_SCALE
            tan = jnp.tanh(part)
            weights = part + part * tan
            sl[p, :, cols] = part
            for m in range(2):
                half = slice(m * T, (m + 1) * T)
                keep = (key_at >= low[pl.ds(u + m, 1), cols]) & (key_at <= high[pl.ds(u + m, 1), cols])
                wt[p, half, cols] = jnp.where(keep, weights[half], 0.0).astype(BF16)
            att_t[:, cols] += dot(values_t, wt[p, :, cols])

    hand_on(0)

    def forward_step(i, _):
        hand_on(i)
        attend(i - 1)
        return 0

    lax.fori_loop(1, 8, forward_step, 0)
    attend(7)

    for k in range(4):
        block = att_t[:, k * T : (k + 1) * T]
        mean = jnp.sum(block, axis=0, keepdims=True) * (1.0 / DH)
        att_s[k, 0:T] = (block - mean).astype(BF16)
        high_part = mean.astype(BF16)
        rest = mean - high_part.astype(F32)
        mid_part = rest.astype(BF16)
        low_part = (rest - mid_part.astype(F32)).astype(BF16)
        r16 = lax.broadcasted_iota(jnp.int32, (16, T), 0)
        att_s[k, T : T + 16] = jnp.where(
            r16 == 0, high_part.astype(F32),
            jnp.where(r16 == 1, mid_part.astype(F32), jnp.where(r16 == 2, low_part.astype(F32), 0.0)),
        ).astype(BF16)
        push(att_s.at[k], ratt.at[hh], att_send.at[k], att_recv.at[hh], k)

    for i in range(1, 4):
        there = 2 * lax.rem(x + i, 4) + c
        arrived(dox.at[there], do_recv.at[there])
        remote(dox.at[there], dox.at[there], do_send.at[3 + i], do_recv.at[there], sib).start()

    def slopes(p, _):
        u = 8 * lax.div(p, 4) + 2 * lax.rem(p, 4)
        key_at = lax.broadcasted_iota(jnp.int32, (T, 256), 0).astype(F32)
        for j in range(2):
            cols = slice(j * 256, (j + 1) * 256)
            for m in range(2):
                half = slice(m * T, (m + 1) * T)
                part = sl[p, half, cols]
                tan = jnp.tanh(part)
                slope = (1.0 + tan) * (HALF_SCALE + (part * HALF_SCALE) * (1.0 - tan))
                keep = (key_at >= low[pl.ds(u + m, 1), cols]) & (key_at <= high[pl.ds(u + m, 1), cols])
                sl[p, half, cols] = jnp.where(keep, slope, 0.0)
        return 0

    lax.fori_loop(0, 8, slopes, 0)

    for h in range(H):
        arrived(ratt.at[h], att_recv.at[h])
    rows = []
    for h in range(H):
        tail = jnp.sum(ratt[h, T : T + 16].astype(F32), axis=0, keepdims=True)
        rows.append(ratt[h, 0:T].astype(F32) + tail)
    mean = sum(jnp.sum(r, axis=0, keepdims=True) for r in rows) * (1.0 / 512)
    rows = [r - mean for r in rows]
    var = sum(jnp.sum(r * r, axis=0, keepdims=True) for r in rows) * (1.0 / 512)
    inv = lax.rsqrt(var + EPS)
    normed = [r * inv for r in rows]
    d_normed = []
    for h in range(H):
        feats = slice(h * DH, (h + 1) * DH)
        gates = gate_t[feats].astype(F32)
        d_gated = dgat[feats]
        gated_t[feats] = (normed[h] * gates).astype(BF16)
        gg_t[feats] = (d_gated * normed[h]).astype(BF16)
        d_normed.append(d_gated * gates)
    mean_d = sum(jnp.sum(d, axis=0, keepdims=True) for d in d_normed) * (1.0 / 512)
    mean_dn = sum(
        jnp.sum(d * n, axis=0, keepdims=True) for d, n in zip(d_normed, normed)
    ) * (1.0 / 512)
    for h in range(H):
        da_s[h] = ((d_normed[h] - mean_d - normed[h] * mean_dn) * inv).astype(BF16)
        push(da_s.at[h], rda.at[hh], da_send.at[h], da_recv.at[hh], h)

    for h in range(H):
        blocks = gated_t[h * DH : (h + 1) * DH].reshape(4, 2, 16, T)
        for cc in range(2):
            g_t[h, cc] = blocks[:, cc]
    g_to = [(x_dev(i, (c + cc) % 2 if cc == 0 else 1 - c), i, cc) for i in range(4) for cc in range(2)][1:]
    for n, (to, i, cc) in enumerate(g_to):
        core = c if cc == 0 else 1 - c
        remote(g_t.at[lax.rem(x + i, 4), core], gx.at[xc], g_send.at[n], g_recv.at[xc], to).start()
    gx[xc] = g_t[x, c]
    for i in range(4):
        theirs = 2 * lax.rem(x + i, 4) + 1 - c
        arrived(dox.at[theirs], do_recv.at[theirs])
        arrived(gx.at[theirs], g_recv.at[theirs])
        if i:
            arrived(gx.at[theirs + 2 * c - 1], g_recv.at[theirs + 2 * c - 1])
    for n in range(2):
        cols = slice(n * 512, (n + 1) * 512)
        part = dot(gx[0].reshape(64, T), dox[0, :, cols])
        for i in range(1, 8):
            part += dot(gx[i].reshape(64, T), dox[i, :, cols])
        wl_f[:, :, cols] = part.reshape(4, 16, 512)
        wl_s[:, :, cols] = part.astype(BF16).reshape(4, 16, 512)
    for i in range(1, 4):
        there = lax.rem(l + i, 4)
        remote(wl_s.at[there], wl_r.at[i - 1], l_send.at[i - 1], l_recv.at[i - 1], l_dev(i)).start()

    for k in range(4):
        arrived(rda.at[k], da_recv.at[k])

    dq_t[...] = jnp.zeros_like(dq_t)

    def back(i):
        k, far = place(7 - i)
        p = 4 * far + k
        values = kv[p, 1]
        d_keys = jnp.zeros((2 * T, DH), F32)
        d_values = jnp.zeros((2 * T, DH), F32)
        for j in range(2):
            cols = slice(j * 256, (j + 1) * 256)
            grads_t = jnp.concatenate([rda[2 * j], rda[2 * j + 1]], axis=1)
            d_scores = (dot(values, grads_t) * sl[p, :, cols]).astype(BF16)
            d_keys += dot(d_scores, rq[2 * j : 2 * j + 2].reshape(256, DH))
            d_values += dot(wt[p, :, cols], grads_t, NT)
            dq_t[:, cols] += dot(kt[p], d_scores)
        dkv_f[i, 0] = d_keys
        dkv_f[i, 1] = d_values
        sib_s[i, 0] = dkv_f[i, 0, sib_rows].astype(BF16)
        sib_s[i, 1] = dkv_f[i, 1, sib_rows].astype(BF16)
        remote(sib_s.at[i], sib_r.at[i], sib_send.at[i], sib_recv.at[i], sib).start()

    def give(i):
        k, far = place(7 - i)
        arrived(sib_r.at[i], sib_recv.at[i])
        dkv_s[i, 0] = (dkv_f[i, 0, own_rows] + sib_r[i, 0].astype(F32)).astype(BF16)
        dkv_s[i, 1] = (dkv_f[i, 1, own_rows] + sib_r[i, 1].astype(F32)).astype(BF16)
        push(
            dkv_s.at[i], rdkv.at[far, hh], dkv_send.at[i], dkv_recv.at[4 * far + hh], k, far == 1
        )

    def back_step(i, _):
        back(i)
        return 0

    def give_step(i, _):
        give(i)
        return 0

    lax.fori_loop(0, 4, back_step, 0)

    total = wl_f[l]
    for i in range(3):
        arrived(wl_r.at[i], l_recv.at[i])
        total += wl_r[i].astype(F32)
    at_near = lax.rem(y, 4)
    near[at_near] = total.astype(BF16)
    for i in range(1, 4):
        remote(near.at[at_near], near.at[at_near], n_send.at[i - 1], n_recv.at[at_near], near_dev(i)).start()

    lax.fori_loop(0, 4, give_step, 0)
    lax.fori_loop(4, 8, back_step, 0)

    def gather_near():
        for i in range(1, 4):
            there = lax.rem(y + i, 4)
            arrived(near.at[there], n_recv.at[there])
        at_far = lax.div(y, 4) * 2 + z
        total = sum(near[i].astype(F32) for i in range(4))
        far_w[at_far] = total.astype(BF16)
        for i in range(1, 4):
            remote(far_w.at[at_far], far_w.at[at_far], f_send.at[i - 1], f_recv.at[at_far], far_dev(i)).start()

    lax.fori_loop(4, 8, give_step, 0)
    for k in range(4):
        dq_s[k] = dq_t[:, k * T : (k + 1) * T].T.astype(BF16)
        push(dq_s.at[k], rdq.at[hh], dq_send.at[k], dq_recv.at[hh], k)

    gather_near()
    lo_v[...] = dot(gated_t[...], w_v[...], TN).astype(BF16)
    for h in range(H):
        feats = slice(h * DH, (h + 1) * DH)
        gg_v[:, feats] = gg_t[feats].T
    outs = [
        pltpu.make_async_copy(src, dst, out_sem.at[i])
        for i, (src, dst) in enumerate((
            (lo_v, lo_out.at[0]), (gg_v, gg_out.at[0]), (dq_v, dq_out.at[0]),
            (dk_v, dk_out.at[0]), (dv_v, dv_out.at[0]), (wa, wg_out),
        ))
    ]
    outs[0].start()
    outs[1].start()

    for h in range(H):
        cols = slice(h * DH, (h + 1) * DH)
        arrived(rdq.at[h], dq_recv.at[h])
        dq_v[:, cols] = rdq[h]
    outs[2].start()
    for h in range(H):
        cols = slice(h * DH, (h + 1) * DH)
        arrived(rdkv.at[0, h], dkv_recv.at[h])
        arrived(rdkv.at[1, h], dkv_recv.at[4 + h])
        dk_v[:, cols] = (rdkv[0, h, 0].astype(F32) + rdkv[1, h, 0].astype(F32)).astype(BF16)
        dv_v[:, cols] = (rdkv[0, h, 1].astype(F32) + rdkv[1, h, 1].astype(F32)).astype(BF16)

    outs[3].start()
    outs[4].start()

    for i in range(1, 4):
        there = lax.rem(lax.div(y, 4) * 2 + z + i, 4)
        arrived(far_w.at[there], f_recv.at[there])
    wa[...] = sum(far_w[i].astype(F32) for i in range(4))
    outs[5].start()

    for k in range(4):
        pushed(q_s.at[k], rq.at[hh], q_send.at[k], q_recv.at[hh], k)
        pushed(att_s.at[k], ratt.at[hh], att_send.at[k], att_recv.at[hh], k)
        pushed(da_s.at[k], rda.at[hh], da_send.at[k], da_recv.at[hh], k)
        pushed(dq_s.at[k], rdq.at[hh], dq_send.at[k], dq_recv.at[hh], k)
        pushed(kv_s.at[k], kv.at[hh, :, my_rows], kv_send.at[k], kv_recv.at[y], k)
        remote(kv_s.at[k], kv.at[hh, :, my_rows], kv_send.at[4 + k], kv_recv.at[y], sib).wait_send()

    def left(i, _):
        here = kv.at[0, :, own_rows]
        remote(here, here, fwd_send.at[i], kv_recv.at[0], sib).wait_send()
        remote(sib_s.at[i], sib_r.at[i], sib_send.at[i], sib_recv.at[i], sib).wait_send()
        k, far = place(7 - i)
        pushed(dkv_s.at[i], rdkv.at[0, hh], dkv_send.at[i], dkv_recv.at[hh], k, far == 1)
        return 0

    lax.fori_loop(0, 8, left, 0)
    for i in range(7):
        remote(dox.at[0], dox.at[0], do_send.at[i], do_recv.at[0], sib).wait_send()
        remote(gx.at[0], gx.at[0], g_send.at[i], g_recv.at[0], sib).wait_send()
    for i in range(3):
        remote(wl_s.at[0], wl_r.at[i], l_send.at[i], l_recv.at[i], sib).wait_send()
        remote(near.at[0], near.at[0], n_send.at[i], n_recv.at[0], sib).wait_send()
        remote(far_w.at[0], far_w.at[0], f_send.at[i], f_recv.at[0], sib).wait_send()

    for copy in outs:
        copy.wait()


def store(*refs):
    ins, outs, held, sem = refs[:6], refs[6:12], refs[12:18], refs[18]
    loads = [pltpu.make_async_copy(ins[i], held[i], sem.at[0, i]) for i in range(6)]
    stores = [pltpu.make_async_copy(held[i], outs[i], sem.at[1, i]) for i in range(6)]
    for copy in loads:
        copy.start()
    for i in range(6):
        loads[i].wait()
        stores[i].start()
    for copy in stores:
        copy.wait()


def body(queries, keys, values, gates, d_out, w_out, lengths, tile_owner, pattern):
    hbm = pl.BlockSpec(memory_space=pl.ANY)
    rows = jax.ShapeDtypeStruct((1, T, 512), BF16)
    outs = (
        jax.ShapeDtypeStruct((1, T, 1024), BF16), rows, rows, rows, rows,
        jax.ShapeDtypeStruct((16, 1024), F32),
    )
    dma = pltpu.SemaphoreType.DMA
    buf = pltpu.VMEM
    scratch = dict(
        lo_v=buf((T, 1024), BF16), dq_v=buf((T, 512), BF16), dk_v=buf((T, 512), BF16),
        dv_v=buf((T, 512), BF16), gg_v=buf((T, 512), BF16),
        kv_s=buf((4, 2, T, DH), BF16), q_s=buf((4, T, DH), BF16), g_v=buf((T, 512), BF16),
        w_v=buf((512, 1024), BF16), len_v=buf((1, 4), jnp.int32), own_v=buf((1, 16), jnp.int32),
        pat_v=buf((1, 16, 16), jnp.int32),
        meta_s=buf((24, 128), F32), meta_r=buf((24, 128), F32),
        kv=buf((8, 2, 2 * T, DH), BF16), rq=buf((4, T, DH), BF16), kt=buf((8, DH, 2 * T), BF16),
        wt=buf((8, 2 * T, 512), BF16), sl=buf((8, 2 * T, 512), F32),
        low=buf((16, 512), F32), high=buf((16, 512), F32),
        att_t=buf((DH, 512), F32), att_s=buf((4, T + 16, DH), BF16), ratt=buf((4, T + 16, DH), BF16),
        dgat=buf((512, T), F32), gate_t=buf((512, T), BF16), gated_t=buf((512, T), BF16),
        gg_t=buf((512, T), BF16),
        da_s=buf((4, T, DH), BF16), rda=buf((4, T, DH), BF16), dkv_f=buf((8, 2, 2 * T, DH), F32),
        sib_s=buf((8, 2, T, DH), BF16), sib_r=buf((8, 2, T, DH), BF16),
        dkv_s=buf((8, 2, T, DH), BF16), rdkv=buf((2, 4, 2, T, DH), BF16),
        dq_t=buf((DH, 512), F32), dq_s=buf((4, T, DH), BF16), rdq=buf((4, T, DH), BF16),
        dox=buf((8, T, 1024), BF16), g_t=buf((4, 2, 4, 16, T), BF16), gx=buf((8, 4, 16, T), BF16),
        wl_f=buf((4, 16, 1024), F32), wl_s=buf((4, 16, 1024), BF16), wl_r=buf((3, 16, 1024), BF16),
        near=buf((4, 16, 1024), BF16), far_w=buf((4, 16, 1024), BF16), wa=buf((16, 1024), F32),
        in_sem=dma((18,)), out_sem=dma((6,)), kv_send=dma((8,)), kv_recv=dma((16,)), fwd_send=dma((8,)),
        q_send=dma((4,)), q_recv=dma((4,)), meta_sem=dma((2,)), att_send=dma((4,)), att_recv=dma((4,)),
        da_send=dma((4,)), da_recv=dma((4,)), sib_send=dma((8,)), sib_recv=dma((8,)),
        dkv_send=dma((8,)), dkv_recv=dma((8,)), dq_send=dma((4,)), dq_recv=dma((4,)),
        do_send=dma((7,)), do_recv=dma((8,)), g_send=dma((7,)), g_recv=dma((8,)),
        l_send=dma((3,)), l_recv=dma((3,)),
        n_send=dma((3,)), n_recv=dma((4,)), f_send=dma((3,)), f_recv=dma((4,)),
    )
    results = pl.pallas_call(
        kernel,
        out_shape=outs,
        in_specs=[hbm] * 9,
        out_specs=(hbm,) * 6,
        scratch_shapes=list(scratch.values()),
        name="hstu",
        compiler_params=pltpu.CompilerParams(
            collective_id=0, has_side_effects=True, vmem_limit_bytes=VMEM
        ),
    )(queries, keys, values, gates, d_out, w_out, lengths, tile_owner, pattern)
    return pl.pallas_call(
        store,
        out_shape=outs,
        in_specs=[hbm] * 6,
        out_specs=(hbm,) * 6,
        scratch_shapes=[buf(o.shape, o.dtype) for o in outs] + [dma((2, 6))],
        name="store",
        compiler_params=pltpu.CompilerParams(vmem_limit_bytes=VMEM),
    )(*results)


def solution(mesh):
    rows = P("dp", "seq", None)
    in_specs = (rows, rows, rows, rows, rows, P(), P("dp", None), P("dp", None), P("dp", None, None))
    out_specs = (rows, rows, rows, rows, rows, P("dp", None))
    return jax.shard_map(body, mesh=mesh, in_specs=in_specs, out_specs=out_specs, check_vma=False)
```

```python
import jax
import jax.numpy as jnp
from jax import lax
from jax.experimental import pallas as pl
from jax.experimental.pallas import tpu as pltpu
from jax.sharding import PartitionSpec as P

H = 4
DH = 128
T = 128
F32 = jnp.float32
BF16 = jnp.bfloat16
MESH = pl.DeviceIdType.MESH
EPS = 1e-06
NT = (((1,), (1,)), ((), ()))
TN = (((0,), (0,)), ((), ()))
VMEM = 60 << 20
HALF_SCALE = 0.5 * DH ** (-0.5)


def dot(a, b, dims=(((1,), (0,)), ((), ()))):
    return lax.dot_general(a, b, dims, preferred_element_type=F32)


def kernel(
    q_ref, k_ref, v_ref, g_ref, do_ref, w_ref, len_ref, own_ref, pat_ref,
    lo_out, dq_out, dk_out, dv_out, gg_out, wg_out,
    lo_v, dq_v, dk_v, dv_v, gg_v, kv_s, q_s, g_v, w_v, len_v, own_v, pat_v,
    meta_s, meta_r, kv, rq, kt, wt, sl, low, high, att_t, att_s, ratt,
    dgat, gate_t, gated_t, gg_t, da_s, rda, dkv_f, sib_s, sib_r, dkv_s, rdkv, dq_t, dq_s, rdq,
    dox, g_t, gx, wl_f, wl_s, wl_r, near, far_w, wa,
    in_sem, out_sem, kv_send, kv_recv, fwd_send, q_send, q_recv, meta_sem, att_send, att_recv,
    da_send, da_recv, sib_send, sib_recv, dkv_send, dkv_recv, dq_send, dq_recv,
    do_send, do_recv, g_send, g_recv, l_send, l_recv, n_send, n_recv, f_send, f_recv,
):
    dp = lax.axis_index("dp")
    sq = lax.axis_index("seq")
    x = lax.div(dp, 8)
    l = lax.rem(lax.div(dp, 2), 4)
    c = lax.rem(dp, 2)
    y = lax.div(sq, 2)
    z = lax.rem(sq, 2)
    par = lax.rem(y, 2)
    hh = lax.div(y, 2)
    xc = x * 2 + c
    sib = (dp + 1 - 2 * c, sq)
    own_par = par == c
    own_rows = pl.ds(pl.multiple_of(c * T, T), T)
    sib_rows = pl.ds(pl.multiple_of((1 - c) * T, T), T)
    my_rows = pl.ds(pl.multiple_of(par * T, T), T)

    def partner(k, far):
        return (dp - c + par, (2 * k + c) * 2 + jnp.where(far, 1 - z, z))

    def is_self(k, far):
        return own_par & (k == hh) & jnp.logical_not(far)

    def remote(src, dst, send, recv, to):
        return pltpu.make_async_remote_copy(
            src_ref=src, dst_ref=dst, send_sem=send, recv_sem=recv, device_id=to,
            device_id_type=MESH,
        )

    def arrived(dst, sem):
        pltpu.make_async_copy(dst, dst, sem).wait()

    def push(src, dst, send, recv, k, far=False):
        if far is True:
            remote(src, dst, send, recv, partner(k, far)).start()
            return
        me = is_self(k, far)

        @pl.when(jnp.logical_not(me))
        def _():
            remote(src, dst, send, recv, partner(k, far)).start()

        @pl.when(me)
        def _():
            pltpu.make_async_copy(src, dst, recv).start()

    def pushed(src, dst, send, recv, k, far=False):
        @pl.when(jnp.logical_not(is_self(k, far)))
        def _():
            remote(src, dst, send, recv, partner(k, far)).wait_send()

    def x_dev(i, cc):
        return (lax.rem(x + i, 4) * 8 + l * 2 + cc, sq)

    def l_dev(i):
        return (x * 8 + lax.rem(l + i, 4) * 2 + c, sq)

    def near_dev(i):
        return (dp, (lax.div(y, 4) * 4 + lax.rem(y + i, 4)) * 2 + z)

    def far_dev(i):
        there = lax.rem(lax.div(y, 4) * 2 + z + i, 4)
        return (dp, (lax.div(there, 2) * 4 + lax.rem(y, 4)) * 2 + lax.rem(there, 2))

    loads = []

    def load(src, dst):
        copy = pltpu.make_async_copy(src, dst, in_sem.at[len(loads)])
        copy.start()
        loads.append(copy)

    load(len_ref, len_v)
    load(own_ref, own_v)
    load(pat_ref, pat_v)
    for h in range(H):
        cols = pl.ds(h * DH, DH)
        load(q_ref.at[0, :, cols], q_s.at[h])
        load(k_ref.at[0, :, cols], kv_s.at[h, 0])
        load(v_ref.at[0, :, cols], kv_s.at[h, 1])
    load(do_ref.at[0], dox.at[xc])
    load(w_ref, w_v)
    load(g_ref.at[0], g_v)

    barrier = pltpu.get_barrier_semaphore()

    def tell(to):
        pl.semaphore_signal(barrier, inc=1, device_id=to, device_id_type=MESH)

    for k in range(4):
        tell(partner(k, True))
        @pl.when(jnp.logical_not(is_self(k, False)))
        def _():
            tell(partner(k, False))
    tell(sib)
    for i in range(1, 4):
        tell(x_dev(i, c))
        tell(x_dev(i, 1 - c))
        tell(l_dev(i))
        tell(near_dev(i))
        tell(far_dev(i))

    for copy in loads[:3]:
        copy.wait()
    meta_s[...] = jnp.zeros_like(meta_s)
    meta_s[0:1, 0:4] = len_v[...].astype(F32)
    meta_s[1:2, 0:16] = own_v[...].astype(F32)
    meta_s[8:24, 0:16] = pat_v[0].astype(F32)
    for copy in loads[3:15]:
        copy.wait()

    pl.semaphore_wait(barrier, 24 - jnp.where(own_par, 1, 0))

    meta_copy = remote(meta_s, meta_r, meta_sem.at[0], meta_sem.at[1], sib)
    meta_copy.start()
    for k in range(4):
        push(q_s.at[k], rq.at[hh], q_send.at[k], q_recv.at[hh], k)
    for k in range(4):
        push(kv_s.at[k], kv.at[4 + hh, :, my_rows], kv_send.at[4 + k], kv_recv.at[8 + y], k, True)
        push(kv_s.at[k], kv.at[hh, :, my_rows], kv_send.at[k], kv_recv.at[y], k)
    for copy in loads[15:]:
        copy.wait()
    remote(dox.at[xc], dox.at[xc], do_send.at[0], do_recv.at[xc], sib).start()
    for i in range(1, 4):
        remote(dox.at[xc], dox.at[xc], do_send.at[i], do_recv.at[xc], x_dev(i, c)).start()

    def place(i):
        step = lax.rem(i, 4)
        turn = jnp.where(step == 2, 3, jnp.where(step == 3, 2, step))
        return lax.rem(hh + turn, 4), lax.div(i, 4)

    dgat[...] = dot(w_v[...], dox[xc], NT)
    for h in range(H):
        gate_t[h * DH : (h + 1) * DH] = g_v[:, h * DH : (h + 1) * DH].T

    meta_copy.wait()
    meta = jnp.where(own_par, meta_s[...], meta_r[...])
    lane = lax.broadcasted_iota(jnp.int32, (16, 128), 1).astype(F32)
    slot = lax.broadcasted_iota(jnp.int32, (16, 128), 0)
    seat = (2 * lax.rem(slot, 8) + jnp.where(slot < 8, z, 1 - z)).astype(F32)
    hot = jnp.where((meta[1:2] == seat) & (lane < 16), 1.0, 0.0)
    tile = jnp.sum(hot * lane, axis=1, keepdims=True)
    col = lax.broadcasted_iota(jnp.int32, (16, 512), 1)
    row = lax.broadcasted_iota(jnp.int32, (16, 512), 0)
    query_hot = jnp.where(row == 2 * lax.div(col, 128) + c, 1.0, 0.0)
    query_tile = jnp.sum(tile * query_hot, axis=0, keepdims=True)
    pos = query_tile * T + lax.rem(col, 128)[0:1].astype(F32)
    upto = slot[0:8].astype(F32)
    lengths = jnp.where((lane[0:8] <= upto) & (lane[0:8] < 4), meta[0:1], 0.0)
    ends = jnp.sum(lengths, axis=1, keepdims=True)
    first = jnp.max(jnp.where(ends <= pos, ends, 0.0), axis=0, keepdims=True)
    tile_hot = jnp.where(row.astype(F32) == query_tile, 1.0, 0.0)
    seen = dot(meta[8:24], tile_hot, TN)
    allow = (dot(hot, seen) > 0.5) | (tile == query_tile)
    low[...] = jnp.where(allow, first - tile * T, 1e6)
    high[...] = pos - tile * T

    for k in range(4):
        arrived(rq.at[k], q_recv.at[k])

    att_t[...] = jnp.zeros_like(att_t)

    def hand_on(i):
        k, far = place(i)
        here = kv.at[4 * far + k, :, own_rows]
        u = 8 * far + 2 * k + c
        arrived(here, kv_recv.at[u])
        remote(here, here, fwd_send.at[i], kv_recv.at[u], sib).start()

    def attend(i):
        k, far = place(i)
        p = 4 * far + k
        u = 8 * far + 2 * k
        arrived(kv.at[p, :, sib_rows], kv_recv.at[u + 1 - c])
        keys = kv[p, 0]
        values_t = kv[p, 1].T
        kt[p] = keys.T
        key_at = lax.broadcasted_iota(jnp.int32, (T, 256), 0).astype(F32)
        for j in range(2):
            cols = slice(j * 256, (j + 1) * 256)
            part = dot(keys, rq[2 * j : 2 * j + 2].reshape(256, DH), NT) * HALF_SCALE
            tan = jnp.tanh(part)
            weights = part + part * tan
            sl[p, :, cols] = part
            for m in range(2):
                half = slice(m * T, (m + 1) * T)
                keep = (key_at >= low[pl.ds(u + m, 1), cols]) & (key_at <= high[pl.ds(u + m, 1), cols])
                wt[p, half, cols] = jnp.where(keep, weights[half], 0.0).astype(BF16)
            att_t[:, cols] += dot(values_t, wt[p, :, cols])

    hand_on(0)

    def forward_step(i, _):
        hand_on(i)
        attend(i - 1)
        return 0

    lax.fori_loop(1, 8, forward_step, 0)
    attend(7)

    for k in range(4):
        block = att_t[:, k * T : (k + 1) * T]
        mean = jnp.sum(block, axis=0, keepdims=True) * (1.0 / DH)
        att_s[k, 0:T] = (block - mean).astype(BF16)
        high_part = mean.astype(BF16)
        rest = mean - high_part.astype(F32)
        mid_part = rest.astype(BF16)
        low_part = (rest - mid_part.astype(F32)).astype(BF16)
        r16 = lax.broadcasted_iota(jnp.int32, (16, T), 0)
        att_s[k, T : T + 16] = jnp.where(
            r16 == 0, high_part.astype(F32),
            jnp.where(r16 == 1, mid_part.astype(F32), jnp.where(r16 == 2, low_part.astype(F32), 0.0)),
        ).astype(BF16)
        push(att_s.at[k], ratt.at[hh], att_send.at[k], att_recv.at[hh], k)

    for i in range(1, 4):
        there = 2 * lax.rem(x + i, 4) + c
        arrived(dox.at[there], do_recv.at[there])
        remote(dox.at[there], dox.at[there], do_send.at[3 + i], do_recv.at[there], sib).start()

    def slopes(p, _):
        u = 8 * lax.div(p, 4) + 2 * lax.rem(p, 4)
        key_at = lax.broadcasted_iota(jnp.int32, (T, 256), 0).astype(F32)
        for j in range(2):
            cols = slice(j * 256, (j + 1) * 256)
            for m in range(2):
                half = slice(m * T, (m + 1) * T)
                part = sl[p, half, cols]
                tan = jnp.tanh(part)
                slope = (1.0 + tan) * (HALF_SCALE + (part * HALF_SCALE) * (1.0 - tan))
                keep = (key_at >= low[pl.ds(u + m, 1), cols]) & (key_at <= high[pl.ds(u + m, 1), cols])
                sl[p, half, cols] = jnp.where(keep, slope, 0.0)
        return 0

    lax.fori_loop(0, 8, slopes, 0)

    for h in range(H):
        arrived(ratt.at[h], att_recv.at[h])
    rows = []
    for h in range(H):
        tail = jnp.sum(ratt[h, T : T + 16].astype(F32), axis=0, keepdims=True)
        rows.append(ratt[h, 0:T].astype(F32) + tail)
    mean = sum(jnp.sum(r, axis=0, keepdims=True) for r in rows) * (1.0 / 512)
    rows = [r - mean for r in rows]
    var = sum(jnp.sum(r * r, axis=0, keepdims=True) for r in rows) * (1.0 / 512)
    inv = lax.rsqrt(var + EPS)
    normed = [r * inv for r in rows]
    d_normed = []
    for h in range(H):
        feats = slice(h * DH, (h + 1) * DH)
        gates = gate_t[feats].astype(F32)
        d_gated = dgat[feats]
        gated_t[feats] = (normed[h] * gates).astype(BF16)
        gg_t[feats] = (d_gated * normed[h]).astype(BF16)
        d_normed.append(d_gated * gates)
    mean_d = sum(jnp.sum(d, axis=0, keepdims=True) for d in d_normed) * (1.0 / 512)
    mean_dn = sum(
        jnp.sum(d * n, axis=0, keepdims=True) for d, n in zip(d_normed, normed)
    ) * (1.0 / 512)
    for h in range(H):
        da_s[h] = ((d_normed[h] - mean_d - normed[h] * mean_dn) * inv).astype(BF16)
        push(da_s.at[h], rda.at[hh], da_send.at[h], da_recv.at[hh], h)

    for h in range(H):
        blocks = gated_t[h * DH : (h + 1) * DH].reshape(4, 2, 16, T)
        for cc in range(2):
            g_t[h, cc] = blocks[:, cc]
    g_to = [(x_dev(i, (c + cc) % 2 if cc == 0 else 1 - c), i, cc) for i in range(4) for cc in range(2)][1:]
    for n, (to, i, cc) in enumerate(g_to):
        core = c if cc == 0 else 1 - c
        remote(g_t.at[lax.rem(x + i, 4), core], gx.at[xc], g_send.at[n], g_recv.at[xc], to).start()
    gx[xc] = g_t[x, c]
    for i in range(4):
        theirs = 2 * lax.rem(x + i, 4) + 1 - c
        arrived(dox.at[theirs], do_recv.at[theirs])
        arrived(gx.at[theirs], g_recv.at[theirs])
        if i:
            arrived(gx.at[theirs + 2 * c - 1], g_recv.at[theirs + 2 * c - 1])
    side = jnp.concatenate([gx[i].reshape(64, T) for i in range(8)], axis=1)
    for n in range(2):
        cols = slice(n * 512, (n + 1) * 512)
        part = dot(side, dox[:, :, cols].reshape(1024, 512))
        wl_f[:, :, cols] = part.reshape(4, 16, 512)
        wl_s[:, :, cols] = part.astype(BF16).reshape(4, 16, 512)
    for i in range(1, 4):
        there = lax.rem(l + i, 4)
        remote(wl_s.at[there], wl_r.at[i - 1], l_send.at[i - 1], l_recv.at[i - 1], l_dev(i)).start()

    for k in range(4):
        arrived(rda.at[k], da_recv.at[k])

    dq_t[...] = jnp.zeros_like(dq_t)

    def back(i):
        k, far = place(7 - i)
        p = 4 * far + k
        values = kv[p, 1]
        d_keys = jnp.zeros((2 * T, DH), F32)
        d_values = jnp.zeros((2 * T, DH), F32)
        for j in range(2):
            cols = slice(j * 256, (j + 1) * 256)
            grads_t = jnp.concatenate([rda[2 * j], rda[2 * j + 1]], axis=1)
            d_scores = (dot(values, grads_t) * sl[p, :, cols]).astype(BF16)
            d_keys += dot(d_scores, rq[2 * j : 2 * j + 2].reshape(256, DH))
            d_values += dot(wt[p, :, cols], grads_t, NT)
            dq_t[:, cols] += dot(kt[p], d_scores)
        dkv_f[i, 0] = d_keys
        dkv_f[i, 1] = d_values
        sib_s[i, 0] = dkv_f[i, 0, sib_rows].astype(BF16)
        sib_s[i, 1] = dkv_f[i, 1, sib_rows].astype(BF16)
        remote(sib_s.at[i], sib_r.at[i], sib_send.at[i], sib_recv.at[i], sib).start()

    def give(i):
        k, far = place(7 - i)
        arrived(sib_r.at[i], sib_recv.at[i])
        dkv_s[i, 0] = (dkv_f[i, 0, own_rows] + sib_r[i, 0].astype(F32)).astype(BF16)
        dkv_s[i, 1] = (dkv_f[i, 1, own_rows] + sib_r[i, 1].astype(F32)).astype(BF16)
        push(
            dkv_s.at[i], rdkv.at[far, hh], dkv_send.at[i], dkv_recv.at[4 * far + hh], k, far == 1
        )

    def back_step(i, _):
        back(i)
        return 0

    def give_step(i, _):
        give(i)
        return 0

    lax.fori_loop(0, 4, back_step, 0)

    total = wl_f[l]
    for i in range(3):
        arrived(wl_r.at[i], l_recv.at[i])
        total += wl_r[i].astype(F32)
    at_near = lax.rem(y, 4)
    near[at_near] = total.astype(BF16)
    for i in range(1, 4):
        remote(near.at[at_near], near.at[at_near], n_send.at[i - 1], n_recv.at[at_near], near_dev(i)).start()

    lax.fori_loop(0, 4, give_step, 0)
    lax.fori_loop(4, 8, back_step, 0)
    def gather_near():
        for i in range(1, 4):
            there = lax.rem(y + i, 4)
            arrived(near.at[there], n_recv.at[there])
        at_far = lax.div(y, 4) * 2 + z
        total = sum(near[i].astype(F32) for i in range(4))
        far_w[at_far] = total.astype(BF16)
        for i in range(1, 4):
            remote(far_w.at[at_far], far_w.at[at_far], f_send.at[i - 1], f_recv.at[at_far], far_dev(i)).start()

    lax.fori_loop(4, 8, give_step, 0)
    for k in range(4):
        dq_s[k] = dq_t[:, k * T : (k + 1) * T].T.astype(BF16)
        push(dq_s.at[k], rdq.at[hh], dq_send.at[k], dq_recv.at[hh], k)

    gather_near()
    lo_v[...] = dot(gated_t[...], w_v[...], TN).astype(BF16)
    for h in range(H):
        feats = slice(h * DH, (h + 1) * DH)
        gg_v[:, feats] = gg_t[feats].T
    outs = [
        pltpu.make_async_copy(src, dst, out_sem.at[i])
        for i, (src, dst) in enumerate((
            (lo_v, lo_out.at[0]), (gg_v, gg_out.at[0]), (dq_v, dq_out.at[0]),
            (dk_v, dk_out.at[0]), (dv_v, dv_out.at[0]), (wa, wg_out),
        ))
    ]
    outs[0].start()
    outs[1].start()

    for h in range(H):
        cols = slice(h * DH, (h + 1) * DH)
        arrived(rdq.at[h], dq_recv.at[h])
        dq_v[:, cols] = rdq[h]
    outs[2].start()
    for h in range(H):
        cols = slice(h * DH, (h + 1) * DH)
        arrived(rdkv.at[0, h], dkv_recv.at[h])
        arrived(rdkv.at[1, h], dkv_recv.at[4 + h])
        dk_v[:, cols] = (rdkv[0, h, 0].astype(F32) + rdkv[1, h, 0].astype(F32)).astype(BF16)
        dv_v[:, cols] = (rdkv[0, h, 1].astype(F32) + rdkv[1, h, 1].astype(F32)).astype(BF16)

    outs[3].start()
    outs[4].start()

    for i in range(1, 4):
        there = lax.rem(lax.div(y, 4) * 2 + z + i, 4)
        arrived(far_w.at[there], f_recv.at[there])
    wa[...] = sum(far_w[i].astype(F32) for i in range(4))
    outs[5].start()

    for k in range(4):
        pushed(q_s.at[k], rq.at[hh], q_send.at[k], q_recv.at[hh], k)
        pushed(att_s.at[k], ratt.at[hh], att_send.at[k], att_recv.at[hh], k)
        pushed(da_s.at[k], rda.at[hh], da_send.at[k], da_recv.at[hh], k)
        pushed(dq_s.at[k], rdq.at[hh], dq_send.at[k], dq_recv.at[hh], k)
        pushed(kv_s.at[k], kv.at[hh, :, my_rows], kv_send.at[k], kv_recv.at[y], k)
        remote(kv_s.at[k], kv.at[hh, :, my_rows], kv_send.at[4 + k], kv_recv.at[y], sib).wait_send()

    def left(i, _):
        here = kv.at[0, :, own_rows]
        remote(here, here, fwd_send.at[i], kv_recv.at[0], sib).wait_send()
        remote(sib_s.at[i], sib_r.at[i], sib_send.at[i], sib_recv.at[i], sib).wait_send()
        k, far = place(7 - i)
        pushed(dkv_s.at[i], rdkv.at[0, hh], dkv_send.at[i], dkv_recv.at[hh], k, far == 1)
        return 0

    lax.fori_loop(0, 8, left, 0)
    for i in range(7):
        remote(dox.at[0], dox.at[0], do_send.at[i], do_recv.at[0], sib).wait_send()
        remote(gx.at[0], gx.at[0], g_send.at[i], g_recv.at[0], sib).wait_send()
    for i in range(3):
        remote(wl_s.at[0], wl_r.at[i], l_send.at[i], l_recv.at[i], sib).wait_send()
        remote(near.at[0], near.at[0], n_send.at[i], n_recv.at[0], sib).wait_send()
        remote(far_w.at[0], far_w.at[0], f_send.at[i], f_recv.at[0], sib).wait_send()

    for copy in outs:
        copy.wait()


def store(*refs):
    ins, outs, held, sem = refs[:6], refs[6:12], refs[12:18], refs[18]
    loads = [pltpu.make_async_copy(ins[i], held[i], sem.at[0, i]) for i in range(6)]
    stores = [pltpu.make_async_copy(held[i], outs[i], sem.at[1, i]) for i in range(6)]
    for copy in loads:
        copy.start()
    for i in range(6):
        loads[i].wait()
        stores[i].start()
    for copy in stores:
        copy.wait()


def body(queries, keys, values, gates, d_out, w_out, lengths, tile_owner, pattern):
    hbm = pl.BlockSpec(memory_space=pl.ANY)
    rows = jax.ShapeDtypeStruct((1, T, 512), BF16)
    outs = (
        jax.ShapeDtypeStruct((1, T, 1024), BF16), rows, rows, rows, rows,
        jax.ShapeDtypeStruct((16, 1024), F32),
    )
    dma = pltpu.SemaphoreType.DMA
    buf = pltpu.VMEM
    scratch = dict(
        lo_v=buf((T, 1024), BF16), dq_v=buf((T, 512), BF16), dk_v=buf((T, 512), BF16),
        dv_v=buf((T, 512), BF16), gg_v=buf((T, 512), BF16),
        kv_s=buf((4, 2, T, DH), BF16), q_s=buf((4, T, DH), BF16), g_v=buf((T, 512), BF16),
        w_v=buf((512, 1024), BF16), len_v=buf((1, 4), jnp.int32), own_v=buf((1, 16), jnp.int32),
        pat_v=buf((1, 16, 16), jnp.int32),
        meta_s=buf((24, 128), F32), meta_r=buf((24, 128), F32),
        kv=buf((8, 2, 2 * T, DH), BF16), rq=buf((4, T, DH), BF16), kt=buf((8, DH, 2 * T), BF16),
        wt=buf((8, 2 * T, 512), BF16), sl=buf((8, 2 * T, 512), F32),
        low=buf((16, 512), F32), high=buf((16, 512), F32),
        att_t=buf((DH, 512), F32), att_s=buf((4, T + 16, DH), BF16), ratt=buf((4, T + 16, DH), BF16),
        dgat=buf((512, T), F32), gate_t=buf((512, T), BF16), gated_t=buf((512, T), BF16),
        gg_t=buf((512, T), BF16),
        da_s=buf((4, T, DH), BF16), rda=buf((4, T, DH), BF16), dkv_f=buf((8, 2, 2 * T, DH), F32),
        sib_s=buf((8, 2, T, DH), BF16), sib_r=buf((8, 2, T, DH), BF16),
        dkv_s=buf((8, 2, T, DH), BF16), rdkv=buf((2, 4, 2, T, DH), BF16),
        dq_t=buf((DH, 512), F32), dq_s=buf((4, T, DH), BF16), rdq=buf((4, T, DH), BF16),
        dox=buf((8, T, 1024), BF16), g_t=buf((4, 2, 4, 16, T), BF16), gx=buf((8, 4, 16, T), BF16),
        wl_f=buf((4, 16, 1024), F32), wl_s=buf((4, 16, 1024), BF16), wl_r=buf((3, 16, 1024), BF16),
        near=buf((4, 16, 1024), BF16), far_w=buf((4, 16, 1024), BF16), wa=buf((16, 1024), F32),
        in_sem=dma((18,)), out_sem=dma((6,)), kv_send=dma((8,)), kv_recv=dma((16,)), fwd_send=dma((8,)),
        q_send=dma((4,)), q_recv=dma((4,)), meta_sem=dma((2,)), att_send=dma((4,)), att_recv=dma((4,)),
        da_send=dma((4,)), da_recv=dma((4,)), sib_send=dma((8,)), sib_recv=dma((8,)),
        dkv_send=dma((8,)), dkv_recv=dma((8,)), dq_send=dma((4,)), dq_recv=dma((4,)),
        do_send=dma((7,)), do_recv=dma((8,)), g_send=dma((7,)), g_recv=dma((8,)),
        l_send=dma((3,)), l_recv=dma((3,)),
        n_send=dma((3,)), n_recv=dma((4,)), f_send=dma((3,)), f_recv=dma((4,)),
    )
    results = pl.pallas_call(
        kernel,
        out_shape=outs,
        in_specs=[hbm] * 9,
        out_specs=(hbm,) * 6,
        scratch_shapes=list(scratch.values()),
        name="hstu",
        compiler_params=pltpu.CompilerParams(
            collective_id=0, has_side_effects=True, vmem_limit_bytes=VMEM
        ),
    )(queries, keys, values, gates, d_out, w_out, lengths, tile_owner, pattern)
    return pl.pallas_call(
        store,
        out_shape=outs,
        in_specs=[hbm] * 6,
        out_specs=(hbm,) * 6,
        scratch_shapes=[buf(o.shape, o.dtype) for o in outs] + [dma((2, 6))],
        name="store",
        compiler_params=pltpu.CompilerParams(vmem_limit_bytes=VMEM),
    )(*results)


def solution(mesh):
    rows = P("dp", "seq", None)
    in_specs = (rows, rows, rows, rows, rows, P(), P("dp", None), P("dp", None), P("dp", None, None))
    out_specs = (rows, rows, rows, rows, rows, P("dp", None))
    return jax.shard_map(body, mesh=mesh, in_specs=in_specs, out_specs=out_specs, check_vma=False)
```
